512 devices in a mesh: seq: 64 (over y, x, core), res: 8 (over z).
Axes of the slice: x: 4, y: 8, z: 8, core: 2. Of those that a mesh axis runs over, the one named last changes fastest.
Arguments:
- alignment: bfloat16 [128, 512, 64], P('seq', 'res'), may hold values from -16 to 16
- cotangent: bfloat16 [128, 512, 64], P('seq', 'res'), may hold values from -6 to 6
- pair_bias: bfloat16 [8, 512, 512], P(None, 'res'), may hold values from -8 to 360
- norm_gains: float32 [2, 64], replicated, may hold values from 0.5 to 1.5
- row_project: float32 [64, 256], replicated, may hold values from -0.75 to 0.75
- row_output: float32 [64, 64], replicated, may hold values from -0.75 to 0.75
- column_project: float32 [64, 144], replicated, may hold values from -16 to 16
- column_output: float32 [64, 64], replicated, may hold values from -0.75 to 0.75
- residue_mask: int32 [512], P('res'), may hold values 0 or 1
- sequence_mask: int32 [128], P('seq'), may hold values from 0 to 1, as said below
Outputs:
- grad_alignment: bfloat16 [128, 512, 64], P('seq', 'res')
- grad_pair_bias: float32 [8, 512, 512], P(None, 'res', 'seq')
- grad_gains: float32 [2, 64], replicated
- grad_row_project: float32 [64, 256], replicated
- grad_row_output: float32 [64, 64], replicated
- grad_column_project: float32 [64, 144], replicated
- grad_column_output: float32 [64, 64], replicated
The draws below stay inside these ranges and needn't reach their ends.
Inputs may be any that keep to these rules, and one draw needn't show every extreme that they name: `sequence_mask`: at least one extra sequence is present.
All inputs are finite; a program needn't handle non-finite values. No bound on the sum of `residue_mask` on one device may be relied on, other than what follows from the above.
Results may differ from the reference program's by a relative error of at most 0.0027.
Values sent between devices are 32-bit elements; how exact they have to be, the bound alone decides.
A program may use at most 128 MiB of HBM per device.

```python
import math
import jax
import jax.numpy as jnp
from jax import lax

C = 64
H = 8
DH = 8
SEQS = 128
RES = 512


def draw_alignment(key, part):
    key = jax.random.fold_in(key, 11)
    noise_part = jax.random.normal(jax.random.fold_in(key, 1), (SEQS, RES, C), jnp.float32)
    values = jnp.clip(noise_part, -8.0, 8.0)
    return values.astype(jnp.bfloat16)


def draw_pair_bias(key, part):
    key = jax.random.fold_in(key, 23)
    values = jnp.clip(1.5 * jax.random.normal(jax.random.fold_in(key, 1), (H, RES, RES), jnp.float32), -8.0, 8.0)
    return values.astype(jnp.bfloat16)


def draw_column_project(key, part):
    key = jax.random.fold_in(key, 37)
    values = jax.random.normal(jax.random.fold_in(key, 1), (C, 2 * C + 2 * DH), jnp.float32) / math.sqrt(C)
    return jnp.clip(values, -16.0, 16.0)


def draw_sequence_mask(key, part):
    key = jax.random.fold_in(key, 41)
    position = jnp.arange(SEQS, dtype=jnp.int32)
    threshold = 250 + 500 * position // SEQS
    rolled = jax.random.randint(key, (SEQS,), 0, 1000)
    present = (rolled < threshold).astype(jnp.int32)
    return jnp.where(position == SEQS - 1, 1, present)


def set_ends(array, stream_key, smallest, high):
    longest = array.shape.index(max(array.shape))
    spots = []
    for shift in (0, 1):
        where = [jax.random.randint(jax.random.fold_in(stream_key, axis), (), 0, length) for axis, length in enumerate(array.shape)]
        where[longest] = (where[longest] + shift) % array.shape[longest]
        spots.append(tuple(where))
    return array.at[spots[0]].set(smallest).at[spots[1]].set(high)


def levels(rng, shape, split, low, high):
    def one(axis_at, blocks):
        draws = jax.random.uniform(jax.random.fold_in(jax.random.fold_in(rng, 6), axis_at), (blocks,), jnp.float32, low / len(split), high / len(split))
        return jnp.repeat(jnp.exp(draws), shape[axis_at] // blocks).reshape((-1,) + (1,) * (len(shape) - axis_at - 1))

    level = one(*split[0])
    for cut in split[1:]:
        level = level * one(*cut)
    return level


def noise(stream_key, shape, deviation, bound, split=(), kind=jnp.bfloat16):
    loudness = levels(stream_key, shape, split, -0.22, 0.18) if split else 1.0
    entries = jax.random.normal(stream_key, shape, jnp.float32) * deviation * loudness
    return jnp.minimum(jnp.maximum(entries, -bound), bound).astype(kind)


def setup_inputs(seed: int = 0) -> dict:
    key_list = jax.random.split(jax.random.key(seed), 11)
    alignment = draw_alignment(jax.random.fold_in(key_list[10], 71), 0)
    cotangent = noise(key_list[1], (SEQS, RES, C), 1.0, 6.0, ((0, 64), (1, 8)))
    pair_bias = draw_pair_bias(jax.random.fold_in(key_list[10], 71), 0)
    norm_gains = jnp.clip(1.0 + 0.1 * jax.random.normal(key_list[3], (2, C), jnp.float32), 0.5, 1.5)
    row_project = noise(key_list[4], (C, 4 * C), C ** -0.5, 0.75, (), jnp.float32)
    row_output = noise(key_list[5], (C, C), C ** -0.5, 0.75, (), jnp.float32)
    column_project = draw_column_project(jax.random.fold_in(key_list[10], 71), 0)
    column_output = noise(key_list[7], (C, C), C ** -0.5, 0.75, (), jnp.float32)
    residue_mask = set_ends((jax.random.randint(key_list[8], (RES,), 0, 8) < 7).astype(jnp.int32), jax.random.fold_in(key_list[8], 1), 0, 1)
    sequence_mask = draw_sequence_mask(jax.random.fold_in(key_list[10], 71), 0)
    return {"alignment": alignment, "cotangent": cotangent, "pair_bias": pair_bias, "norm_gains": norm_gains, "row_project": row_project, "row_output": row_output, "column_project": column_project, "column_output": column_output, "residue_mask": residue_mask, "sequence_mask": sequence_mask}


PRECISE = lax.Precision.HIGHEST
EPSILON = 1e-05
MASKED = 1000000000.0

def layer_norm(values, gain_vector):
    centre = lax.optimization_barrier(jnp.mean(values, axis=-1, keepdims=True))
    centred = values - centre
    spread = lax.optimization_barrier(jnp.mean(centred * centred, axis=-1, keepdims=True))
    return centred * lax.rsqrt(spread + EPSILON) * gain_vector

def row_single(normed, row_project, row_output, bias_values, key_bias):
    projected = jnp.dot(normed, row_project, precision=PRECISE)
    queries = projected[:, :C].reshape(-1, H, DH) * DH ** (-0.5)
    key_rows = projected[:, C:2 * C].reshape(-1, H, DH)
    value_rows = projected[:, 2 * C:3 * C].reshape(-1, H, DH)
    gating = jax.nn.sigmoid(projected[:, 3 * C:])
    scores = jnp.einsum('qhd,khd->hqk', queries, key_rows, precision=PRECISE) + bias_values + key_bias[None, None, :]
    weights = jax.nn.softmax(scores, axis=-1)
    mixture = jnp.einsum('hqk,khd->qhd', weights, value_rows, precision=PRECISE).reshape(-1, C)
    return jnp.dot(gating * mixture, row_output, precision=PRECISE)

def column_global(normed, present, column_project, column_output):
    counted = jnp.sum(present)
    mean_normed = jnp.einsum('s,src->rc', present, normed, precision=PRECISE) / counted
    queries = jnp.dot(mean_normed, column_project[:, :C], precision=PRECISE).reshape(-1, H, DH) * DH ** (-0.5)
    key_rows = jnp.einsum('src,cd->srd', normed, column_project[:, C:C + DH], precision=PRECISE)
    value_rows = jnp.einsum('src,cd->srd', normed, column_project[:, C + DH:C + 2 * DH], precision=PRECISE)
    gating = jax.nn.sigmoid(jnp.einsum('src,cd->srd', normed, column_project[:, C + 2 * DH:], precision=PRECISE))
    scores = jnp.einsum('rhd,srd->srh', queries, key_rows, precision=PRECISE) + MASKED * (present - 1.0)[:, None, None]
    weights = jax.nn.softmax(scores, axis=0)
    mixture = jnp.einsum('srh,srd->rhd', weights, value_rows, precision=PRECISE).reshape(-1, C)
    return jnp.einsum('src,cd->srd', gating * mixture[None], column_output, precision=PRECISE)

def reference(alignment, cotangent, pair_bias, norm_gains, row_project, row_output, column_project, column_output, residue_mask, sequence_mask):
    key_bias = MASKED * (residue_mask.astype(jnp.float32) - 1.0)
    present = sequence_mask.astype(jnp.float32)
    row_step = jax.checkpoint(row_single)

    def forward(initial, bias_values, gains, row_weights, row_out_weights, column_weights, column_out_weights):
        normed = layer_norm(initial, gains[0])
        row_result = lax.map(lambda normed_row: row_step(normed_row, row_weights, row_out_weights, bias_values, key_bias), normed)
        middle = initial + row_result
        return middle + column_global(layer_norm(middle, gains[1]), present, column_weights, column_out_weights)
    primals = (alignment.astype(jnp.float32), pair_bias.astype(jnp.float32), norm_gains, row_project, row_output, column_project, column_output)
    outcome, backward = jax.vjp(forward, *primals)
    gradients = backward(cotangent.astype(jnp.float32))
    return (gradients[0].astype(jnp.bfloat16), gradients[1], gradients[2], gradients[3], gradients[4], gradients[5], gradients[6])
```

```python
import functools
import jax
import jax.numpy as jnp
from jax import lax
from jax.experimental import pallas as pl
from jax.experimental.pallas import tpu as pltpu
from jax.sharding import PartitionSpec as P

C = 64
H = 8
DH = 8
L = 2
PAIRS = 4
W = 128
EPSILON = 1e-05
MASKED = 1000000000.0
F32 = jnp.float32
BF16 = jnp.bfloat16
MESH = pl.DeviceIdType.MESH
NN = (((1,), (0,)), ((), ()))
NT = (((1,), (1,)), ((), ()))
TN = (((0,), (0,)), ((), ()))


def dot(a, b, dims=NN):
    return lax.dot_general(
        a, b, dims, precision=lax.Precision.HIGHEST, preferred_element_type=F32
    )


def dot1(a, b, dims=NN):
    return lax.dot_general(a, b, dims, preferred_element_type=F32)


def split2(a):
    high = a.astype(BF16)
    return high, (a - high.astype(F32)).astype(BF16)


def split3(a):
    high = a.astype(BF16)
    rest = a - high.astype(F32)
    middle = rest.astype(BF16)
    return high, middle, (rest - middle.astype(F32)).astype(BF16)


def dot3(a, b, dims=NN):
    ah, al = split2(a)
    bh, bl = split2(b)
    return dot1(ah, bh, dims) + (dot1(ah, bl, dims) + dot1(al, bh, dims))


def iota(shape, axis):
    return lax.broadcasted_iota(jnp.int32, shape, axis)


def ones_where(condition):
    return jnp.where(condition, 1.0, 0.0).astype(F32)


def twice(row):
    return jnp.concatenate([row, row], axis=1)


def fold(row):
    return row + jnp.concatenate([row[:, C:], row[:, :C]], axis=1)


def block_diagonal(weights):
    zero = jnp.zeros_like(weights)
    return jnp.concatenate(
        [jnp.concatenate([weights, zero], axis=1), jnp.concatenate([zero, weights], axis=1)], axis=0
    )


def diagonal_sum(full):
    return full[:C, :C] + full[C:, C:]


def kernel(
    sizes,
    align_ref,
    cot_ref,
    bias_ref,
    gains_ref,
    rowp_ref,
    rowo_ref,
    colp_ref,
    colo_ref,
    rmask_ref,
    smask_ref,
    galign_ref,
    gbias_ref,
    ggains_ref,
    growp_ref,
    growo_ref,
    gcolp_ref,
    gcolo_ref,
    xall,
    gsend,
    grecv,
    msend,
    mrecv,
    bsend,
    brecv,
    bias_t,
    exps,
    bias_s,
    core_r,
    x_s,
    x_r,
    y_s,
    y_r,
    zr_s,
    zr_r,
    pc_s,
    pc_r,
    pr_s,
    pr_r,
    t_s,
    t_r,
    o_r,
    send_sem,
    recv_sem,
    bias_send,
    bias_recv,
):
    ny, nx, nz = sizes
    ns = ny * nx * 2
    res = ns
    keys = nz * res
    wide = 4 * res
    half = 2 * res
    block = keys // ns
    me = lax.axis_index("seq")
    mz = lax.axis_index("res")
    core = lax.rem(me, 2)
    mx = lax.rem(me // 2, nx)
    my = me // (2 * nx)
    scaling = DH ** (-0.5)

    barrier = pltpu.get_barrier_semaphore()

    def greet_seq(i, carry):
        pl.semaphore_signal(
            barrier, inc=1, device_id=(lax.rem(me + i, ns), mz), device_id_type=MESH
        )
        return carry

    def greet_res(i, carry):
        pl.semaphore_signal(
            barrier, inc=1, device_id=(me, lax.rem(mz + i, nz)), device_id_type=MESH
        )
        return carry

    lax.fori_loop(1, nz, greet_res, 0)
    lax.fori_loop(1, ns, greet_seq, 0)

    def to_seq(source, target, which):
        def one(i, carry):
            j = lax.rem(me + i, ns)
            pltpu.make_async_remote_copy(
                src_ref=source(j),
                dst_ref=target.at[me],
                send_sem=send_sem.at[which],
                recv_sem=recv_sem.at[which],
                device_id=(j, mz),
                device_id_type=MESH,
            ).start()
            return carry

        lax.fori_loop(1, ns, one, 0)

    def to_res(source, target, which):
        def one(i, carry):
            j = lax.rem(mz + i, nz)
            pltpu.make_async_remote_copy(
                src_ref=source(j),
                dst_ref=target.at[mz],
                send_sem=send_sem.at[which],
                recv_sem=recv_sem.at[which],
                device_id=(me, j),
                device_id_type=MESH,
            ).start()
            return carry

        lax.fori_loop(1, nz, one, 0)

    def wait(ref, semaphore):
        pltpu.make_async_copy(ref, ref, semaphore).wait()

    def wait_all(buffer, which, count):
        part = buffer.at[pl.ds(0, count - 1)]
        wait(part, recv_sem.at[which])
        wait(part, send_sem.at[which])

    def keep(source, target, at):
        target[pl.ds(at, 1)] = source[pl.ds(at, 1)]

    align = align_ref[...].astype(F32)
    initial = jnp.concatenate([align[0], align[1]], axis=1)
    cot = cot_ref[...].astype(F32)
    top_local = jnp.concatenate([cot[0], cot[1]], axis=1)
    gains = gains_ref[...]
    gain_row = twice(gains[0:1])
    gain_col = twice(gains[1:2])
    averaging = ones_where(iota((W, W), 0) // C == iota((W, W), 1) // C) * (1.0 / C)

    def layer_norm(values):
        centred = values - dot(values, averaging)
        spread = dot(centred * centred, averaging)
        inverse = lax.rsqrt(spread + EPSILON)
        return centred * inverse, inverse

    def layer_norm_back(grad_normed, gain, hat, inverse):
        scaled = grad_normed * gain
        rows = scaled.shape[0]
        means = dot(jnp.concatenate([scaled, scaled * hat], axis=0), averaging)
        return inverse * (scaled - means[:rows] - hat * means[rows:])

    hat_local, inverse_local = layer_norm(initial)
    xall[mz, 0:res, :] = hat_local
    xall[mz, res : res + 8, :] = jnp.broadcast_to(rmask_ref[...].astype(F32), (8, W))
    present_row = smask_ref[...].astype(F32)
    gsend[:, 0, 0:W] = top_local
    gsend[:, 0, W : 2 * W] = jnp.broadcast_to(present_row, (res, W))

    pl.semaphore_wait(barrier, ns + nz - 2)
    to_res(lambda j: xall.at[mz], xall, 0)
    to_seq(lambda j: gsend.at[j], grecv, 1)
    keep(gsend, grecv, me)

    lane = iota((C, W), 1)
    column = (lane // 32) * 16 + lane % 16
    chosen = [
        ones_where((iota((C, W), 0) == column) & ((lane // 16) % 2 == s)) for s in range(L)
    ]

    def spread_columns(weights):
        return jnp.concatenate([dot(weights, chosen[0]), dot(weights, chosen[1])], axis=0)

    def gather_columns(full):
        return dot(full[:C], chosen[0], NT) + dot(full[C:], chosen[1], NT)

    rowp = rowp_ref[...]
    query_w = spread_columns(rowp[:, 0:C])
    key_w = spread_columns(rowp[:, C : 2 * C])
    value_w = spread_columns(rowp[:, 2 * C : 3 * C])
    gate_w = spread_columns(rowp[:, 3 * C :])
    rowo = rowo_ref[...]
    out_w = jnp.concatenate([dot(chosen[0], rowo, TN), dot(chosen[1], rowo, TN)], axis=1)
    memory_w = jnp.concatenate([key_w, value_w], axis=1)

    normed_local = hat_local * gain_row
    queries = dot(normed_local, query_w) * scaling
    gate_row = jax.nn.sigmoid(dot(normed_local, gate_w))

    for p in range(PAIRS):
        pair = bias_ref[2 * p : 2 * p + 2].astype(F32).reshape(half, keys)
        bias_t[p] = pair.T

    match = iota((W, wide), 0) // DH - iota((W, wide), 1) // res

    def heads_apart(rows):
        flat = rows.T
        flat = jnp.concatenate([flat, flat, flat, flat], axis=1)
        return [jnp.where(match == 4 * p, flat, 0.0) for p in range(PAIRS)]

    queries_apart = heads_apart(queries)
    query_terms = []
    for p in range(PAIRS):
        q1, q2, q3 = split3(queries_apart[p])
        query_terms.append(
            (
                jnp.concatenate([q1, q1], axis=0),
                jnp.concatenate([q2, q2], axis=0),
                jnp.concatenate([q3, q1], axis=0),
            )
        )

    mine = ones_where(iota((32, wide), 0) // DH == iota((32, wide), 1) // res)

    def heads_together(apart):
        kept = apart * mine
        both = kept[:, :half] + kept[:, half:]
        return both[:, :res] + both[:, res:]

    colp = colp_ref[...]
    colo = colo_ref[...]
    entry = iota((C + 2 * DH + C, C), 0)
    entry_lane = iota((C + 2 * DH + C, C), 1)
    key_col_w = block_diagonal(dot(colp, ones_where(entry == C + entry_lane % DH)))
    value_col_w = block_diagonal(dot(colp, ones_where(entry == C + DH + entry_lane % DH)))
    gate_col_w = block_diagonal(dot(colp, ones_where(entry == C + 2 * DH + entry_lane)))
    query_col_w = block_diagonal(colp[:, 0:C])
    out_col_w = block_diagonal(colo)
    column_w = jnp.concatenate([key_col_w, value_col_w, gate_col_w], axis=1)
    head_sum = ones_where(iota((W, W), 0) // DH == iota((W, W), 1) // DH)

    wait_all(xall, 0, nz)
    hat_all = xall[:, 0:res, :].reshape(keys, W)
    normed_all = hat_all * gain_row
    memory = dot(normed_all, memory_w)
    key_rows = memory[:, :W]
    value_rows = memory[:, W:]
    value_flat = value_rows.T
    mask_flat = jnp.concatenate([xall[z, res : res + 8, :] for z in range(nz)], axis=0).T
    key_bias = jnp.concatenate(
        [MASKED * (mask_flat[:res, 8 * z : 8 * z + 1] - 1.0) for z in range(nz)], axis=0
    )
    k1, k2, k3 = split3(key_rows)
    k12 = jnp.concatenate([k1, k2], axis=1)
    k13 = jnp.concatenate([k1, k3], axis=1)
    value_high, value_low = split2(value_flat)

    totals = []
    mixed = []
    for p in range(PAIRS):
        terms = query_terms[p]
        scores = dot1(k12, terms[0]) + (dot1(k12, terms[1]) + dot1(k13, terms[2]))
        scores = scores + twice(bias_t[p]) + key_bias
        peak = jnp.max(scores, axis=0, keepdims=True)
        exponent = jnp.exp(scores - peak)
        exps[p] = exponent
        inverse_total = 1.0 / jnp.sum(exponent, axis=0, keepdims=True)
        totals.append(inverse_total)
        eh, el = split2(exponent)
        vh = value_high[32 * p : 32 * p + 32]
        vl = value_low[32 * p : 32 * p + 32]
        apart = dot1(vh, eh) + (dot1(vl, eh) + dot1(vh, el))
        mixed.append(heads_together(apart * inverse_total))
    mixture = jnp.concatenate(mixed, axis=0).T
    gated = gate_row * mixture
    middle = initial + dot(gated, out_w)
    msend[:, 0, :] = middle
    to_seq(lambda j: msend.at[j], mrecv, 2)
    keep(msend, mrecv, me)

    wait_all(grecv, 1, ns)
    top = grecv[:, 0, 0:W]
    present = grecv[:, 0, W : 2 * W]
    counted = jnp.sum(fold(jnp.sum(present, axis=0, keepdims=True)), axis=1, keepdims=True) * (
        1.0 / W
    )
    inverse_count = 1.0 / counted
    grad_gated_col = dot(top, out_col_w, NT)

    wait_all(mrecv, 2, ns)
    hat_col, inverse_col = layer_norm(mrecv[:, 0, :])
    normed_col = hat_col * gain_col
    mean_normed = fold(jnp.sum(present * normed_col, axis=0, keepdims=True)) * inverse_count
    queries_col = dot(mean_normed, query_col_w) * scaling
    projected = dot(normed_col, column_w)
    key_col = projected[:, 0:W]
    value_col = projected[:, W : 2 * W]
    gate_col = jax.nn.sigmoid(projected[:, 2 * W :])
    scores_col = dot(key_col * queries_col, head_sum) + MASKED * (present - 1.0)
    peak_row = jnp.max(scores_col, axis=0, keepdims=True)
    peak_row = jnp.maximum(peak_row, jnp.concatenate([peak_row[:, C:], peak_row[:, :C]], axis=1))
    exp_col = jnp.exp(scores_col - peak_row)
    weights_col = exp_col * (1.0 / fold(jnp.sum(exp_col, axis=0, keepdims=True)))
    mixture_col = fold(jnp.sum(weights_col * value_col, axis=0, keepdims=True))
    grad_mixture_col = fold(jnp.sum(gate_col * grad_gated_col, axis=0, keepdims=True))
    grad_gate_col = grad_gated_col * mixture_col * gate_col * (1.0 - gate_col)
    grad_weights_col = dot(value_col * grad_mixture_col, head_sum)
    inner_col = fold(jnp.sum(weights_col * grad_weights_col, axis=0, keepdims=True))
    grad_scores_col = weights_col * (grad_weights_col - inner_col)
    grad_query_col = fold(jnp.sum(grad_scores_col * key_col, axis=0, keepdims=True)) * scaling
    grad_key_col = grad_scores_col * queries_col
    grad_value_col = weights_col * grad_mixture_col
    grad_mean = dot(grad_query_col, query_col_w, NT)
    grad_projected = jnp.concatenate([grad_key_col, grad_value_col, grad_gate_col], axis=1)
    grad_normed_col = present * inverse_count * grad_mean + dot(grad_projected, column_w, NT)
    grad_middle_col = top + layer_norm_back(grad_normed_col, gain_col, hat_col, inverse_col)
    bsend[:, 0, :] = grad_middle_col
    to_seq(lambda j: bsend.at[j], brecv, 3)
    keep(bsend, brecv, me)

    pack_lane = iota((C, 2 * W), 1)
    pack_row = iota((C, 2 * W), 0)
    grad_full = dot(normed_col, grad_projected, TN)
    identity = ones_where(iota((C, C), 0) == iota((C, C), 1))
    mean_column = jnp.sum(identity * mean_normed[:, :C], axis=1, keepdims=True)
    grad_col_parts = jnp.concatenate(
        [
            mean_column * grad_query_col[:, :C],
            diagonal_sum(grad_full[:, 0:W]),
            diagonal_sum(grad_full[:, W : 2 * W]),
            diagonal_sum(grad_full[:, 2 * W :]),
            diagonal_sum(dot(gate_col * mixture_col, top, TN)),
        ],
        axis=1,
    )
    placing = jnp.concatenate(
        [
            ones_where(pack_lane == pack_row),
            ones_where(pack_lane == C + pack_row % DH),
            ones_where(pack_lane == C + DH + pack_row % DH),
            ones_where(pack_lane == C + 2 * DH + pack_row),
            ones_where(pack_lane == 2 * C + 2 * DH + pack_row),
        ],
        axis=0,
    )
    gain_sums = fold(jnp.sum(grad_normed_col * hat_col, axis=0, keepdims=True))
    gain_column = jnp.sum(identity * gain_sums[:, :C], axis=1, keepdims=True)
    pack = dot(grad_col_parts, placing) + jnp.where(
        pack_lane == 3 * C + 2 * DH, gain_column, 0.0
    )
    pc_s[...] = pack.reshape(ns, C // ns, 2 * W)
    to_seq(lambda j: pc_s.at[j], pc_r, 4)
    keep(pc_s, pc_r, me)

    key_flat = key_rows.T
    key_high, key_low = split2(key_flat)
    v1, v2 = split2(value_rows)
    v12 = jnp.concatenate([v1, v2], axis=1)

    wait_all(brecv, 3, ns)
    grad_middle = brecv[:, 0, :]
    grad_gated = dot(grad_middle, out_w, NT)
    grad_gate = grad_gated * mixture * gate_row * (1.0 - gate_row)
    grads_apart = heads_apart(grad_gated * gate_row)

    def bias_core(p):
        return pltpu.make_async_remote_copy(
            src_ref=bias_s.at[p, :, :, 1 - core],
            dst_ref=core_r.at[p],
            send_sem=bias_send.at[0, p],
            recv_sem=bias_recv.at[0, p],
            device_id=(me + 1 - 2 * core, mz),
            device_id_type=MESH,
        )

    def bias_to_x(p):
        bias_core(p).wait()
        x_s[p] = jnp.swapaxes(bias_s[p, :, :, core] + core_r[p], 0, 1)

        def one(i, carry):
            j = lax.rem(mx + i, nx)
            pltpu.make_async_remote_copy(
                src_ref=x_s.at[p, j],
                dst_ref=x_r.at[p, mx],
                send_sem=bias_send.at[1, p],
                recv_sem=bias_recv.at[1, p],
                device_id=((my * nx + j) * 2 + core, mz),
                device_id_type=MESH,
            ).start()
            return carry

        lax.fori_loop(1, nx, one, 0)
        x_r[p, pl.ds(mx, 1)] = x_s[p, pl.ds(mx, 1)]

    def bias_to_y(p):
        part = x_r.at[p, pl.ds(0, nx - 1)]
        wait(part, bias_recv.at[1, p])
        wait(part, bias_send.at[1, p])
        y_s[p] = sum([x_r[p, i] for i in range(1, nx)], x_r[p, 0])

        def one(i, carry):
            j = lax.rem(my + i, ny)
            pltpu.make_async_remote_copy(
                src_ref=y_s.at[p, j],
                dst_ref=y_r.at[p, my],
                send_sem=bias_send.at[2, p],
                recv_sem=bias_recv.at[2, p],
                device_id=((j * nx + mx) * 2 + core, mz),
                device_id_type=MESH,
            ).start()
            return carry

        lax.fori_loop(1, ny, one, 0)
        y_r[p, pl.ds(my, 1)] = y_s[p, pl.ds(my, 1)]

    def bias_done(p):
        part = y_r.at[p, pl.ds(0, ny - 1)]
        wait(part, bias_recv.at[2, p])
        wait(part, bias_send.at[2, p])
        total = sum([y_r[p, i] for i in range(1, ny)], y_r[p, 0])
        flat = total.T
        gbias_ref[2 * p] = flat[:res]
        gbias_ref[2 * p + 1] = flat[res:]

    grad_keys = jnp.zeros((keys, W), F32)
    grad_values = jnp.zeros((keys, W), F32)
    grad_queries = []
    for p in range(PAIRS):
        gh, gl = split2(grads_apart[p])
        grad_weights = dot1(v12, jnp.concatenate([gh, gh], axis=0)) + dot1(v1, gl)
        weights = exps[p] * totals[p]
        inner = jnp.sum(weights * grad_weights, axis=0, keepdims=True)
        grad_scores = weights * (grad_weights - inner)
        bias_s[p] = (grad_scores[:, :half] + grad_scores[:, half:]).reshape(
            ny, nx, 2, block, half
        )
        bias_core(p).start()
        sh, sl = split2(grad_scores)
        wh, wl = split2(weights)
        q1, q2 = split2(queries_apart[p])
        grad_keys = grad_keys + (dot1(sh, q1, NT) + (dot1(sh, q2, NT) + dot1(sl, q1, NT)))
        grad_values = grad_values + (dot1(wh, gh, NT) + (dot1(wh, gl, NT) + dot1(wl, gh, NT)))
        kh = key_high[32 * p : 32 * p + 32]
        kl = key_low[32 * p : 32 * p + 32]
        grad_queries.append(
            heads_together(dot1(kh, sh) + (dot1(kl, sh) + dot1(kh, sl)))
        )
        if p >= 1:
            bias_to_x(p - 1)
        if p >= 2:
            bias_to_y(p - 2)

    grad_memory = jnp.concatenate([grad_keys, grad_values], axis=1)
    partial = dot3(grad_memory, memory_w, NT)
    zr_s[...] = partial.reshape(nz, res, W)
    to_res(lambda j: zr_s.at[j], zr_r, 5)
    keep(zr_s, zr_r, mz)
    bias_to_x(PAIRS - 1)

    grad_query = jnp.concatenate(grad_queries, axis=0).T * scaling
    own_grads = jnp.concatenate([grad_query, grad_gate], axis=1)
    own_weights = jnp.concatenate([query_w, gate_w], axis=1)
    own_normed_grad = dot(own_grads, own_weights, NT)
    grad_memory_w = dot3(normed_all, grad_memory, TN)
    grad_own_w = dot(normed_local, own_grads, TN)
    grad_out_w = dot(gated, grad_middle, TN)
    gain_sums_row = fold(
        jnp.sum(partial * hat_all, axis=0, keepdims=True)
        + jnp.sum(own_normed_grad * hat_local, axis=0, keepdims=True)
    )
    gain_column_row = jnp.sum(identity * gain_sums_row[:, :C], axis=1, keepdims=True)
    grad_rowo = dot(chosen[0], grad_out_w[:, :C]) + dot(chosen[1], grad_out_w[:, C:])
    pack_row_part = jnp.concatenate(
        [
            gather_columns(grad_own_w[:, :W]),
            gather_columns(grad_memory_w[:, :W]),
            gather_columns(grad_memory_w[:, W:]),
            gather_columns(grad_own_w[:, W:]),
            grad_rowo,
            jnp.broadcast_to(gain_column_row, (C, C)),
        ],
        axis=1,
    )
    pr_s[...] = pack_row_part.reshape(ns, C // ns, 3 * W)
    to_seq(lambda j: pr_s.at[j], pr_r, 6)
    keep(pr_s, pr_r, me)
    bias_to_y(PAIRS - 2)

    wait_all(pc_r, 4, ns)
    wait_all(pr_r, 6, ns)
    t_s[...] = jnp.concatenate(
        [jnp.sum(pr_r[...], axis=0), jnp.sum(pc_r[...], axis=0)], axis=1
    )
    to_res(lambda j: t_s, t_r, 7)
    t_r[pl.ds(mz, 1)] = t_s[...][None]
    bias_to_y(PAIRS - 1)

    wait_all(zr_r, 5, nz)
    grad_normed_row = sum([zr_r[i] for i in range(1, nz)], zr_r[0]) + own_normed_grad
    grad_initial = layer_norm_back(grad_normed_row, gain_row, hat_local, inverse_local)
    grad_align = (grad_middle + grad_initial).astype(BF16)
    galign_ref[0] = grad_align[:, :C]
    galign_ref[1] = grad_align[:, C:]

    wait_all(t_r, 7, nz)
    o_r[me] = sum([t_r[i] for i in range(1, nz)], t_r[0])
    to_seq(lambda j: o_r.at[me], o_r, 8)
    for p in range(PAIRS):
        bias_done(p)
    wait_all(o_r, 8, ns)
    final = o_r[...].reshape(C, 5 * W)
    growp_ref[...] = final[:, 0 : 4 * C]
    growo_ref[...] = final[:, 4 * C : 5 * C]
    column_part = final[:, 3 * W :]
    gcolp_ref[...] = column_part[:, 0 : 2 * C + 2 * DH]
    gcolo_ref[...] = column_part[:, 2 * C + 2 * DH : 3 * C + 2 * DH]
    row_gain = final[:, 2 * W : 3 * W].T[C : C + 1]
    col_gain = column_part[:, W:].T[3 * C + 2 * DH - W : 3 * C + 2 * DH - W + 1]
    ggains_ref[0:1, :] = row_gain
    ggains_ref[1:2, :] = col_gain


def solution(mesh):
    seq_devices = mesh.shape["seq"]
    res_devices = mesh.shape["res"]
    nx = 4 if seq_devices == 64 else 2
    ny = seq_devices // (2 * nx)
    nz = res_devices
    res = seq_devices
    keys = nz * res
    block = keys // seq_devices
    half = 2 * res

    def local(
        alignment,
        cotangent,
        pair_bias,
        norm_gains,
        row_project,
        row_output,
        column_project,
        column_output,
        residue_mask,
        sequence_mask,
    ):
        rmask = jnp.pad(residue_mask[None], ((0, 0), (0, W - res)))
        smask = jnp.repeat(sequence_mask, C)[None]
        vmem = pl.BlockSpec(memory_space=pltpu.VMEM)
        ns = seq_devices
        chunk = C // ns
        return pl.pallas_call(
            functools.partial(kernel, (ny, nx, nz)),
            out_shape=(
                jax.ShapeDtypeStruct((L, res, C), BF16),
                jax.ShapeDtypeStruct((H, res, block), F32),
                jax.ShapeDtypeStruct((2, C), F32),
                jax.ShapeDtypeStruct((C, 4 * C), F32),
                jax.ShapeDtypeStruct((C, C), F32),
                jax.ShapeDtypeStruct((C, 2 * C + 2 * DH), F32),
                jax.ShapeDtypeStruct((C, C), F32),
            ),
            in_specs=[vmem] * 10,
            out_specs=(vmem,) * 7,
            scratch_shapes=[
                pltpu.VMEM((nz, res + 8, W), F32),
                pltpu.VMEM((ns, 1, 2 * W), F32),
                pltpu.VMEM((ns, 1, 2 * W), F32),
                pltpu.VMEM((ns, 1, W), F32),
                pltpu.VMEM((ns, 1, W), F32),
                pltpu.VMEM((ns, 1, W), F32),
                pltpu.VMEM((ns, 1, W), F32),
                pltpu.VMEM((PAIRS, keys, half), F32),
                pltpu.VMEM((PAIRS, keys, 2 * half), F32),
                pltpu.VMEM((PAIRS, ny, nx, 2, block, half), F32),
                pltpu.VMEM((PAIRS, ny, nx, block, half), F32),
                pltpu.VMEM((PAIRS, nx, ny, block, half), F32),
                pltpu.VMEM((PAIRS, nx, ny, block, half), F32),
                pltpu.VMEM((PAIRS, ny, block, half), F32),
                pltpu.VMEM((PAIRS, ny, block, half), F32),
                pltpu.VMEM((nz, res, W), F32),
                pltpu.VMEM((nz, res, W), F32),
                pltpu.VMEM((ns, chunk, 2 * W), F32),
                pltpu.VMEM((ns, chunk, 2 * W), F32),
                pltpu.VMEM((ns, chunk, 3 * W), F32),
                pltpu.VMEM((ns, chunk, 3 * W), F32),
                pltpu.VMEM((chunk, 5 * W), F32),
                pltpu.VMEM((nz, chunk, 5 * W), F32),
                pltpu.VMEM((ns, chunk, 5 * W), F32),
                pltpu.SemaphoreType.DMA((9,)),
                pltpu.SemaphoreType.DMA((9,)),
                pltpu.SemaphoreType.DMA((3, PAIRS)),
                pltpu.SemaphoreType.DMA((3, PAIRS)),
            ],
            compiler_params=pltpu.CompilerParams(
                collective_id=0, has_side_effects=True, vmem_limit_bytes=48 * 1024 * 1024
            ),
        )(
            alignment,
            cotangent,
            pair_bias,
            norm_gains,
            row_project,
            row_output,
            column_project,
            column_output,
            rmask,
            smask,
        )

    placed = (
        P("seq", "res", None),
        P("seq", "res", None),
        P(None, "res", None),
        P(),
        P(),
        P(),
        P(),
        P(),
        P("res"),
        P("seq"),
    )
    return jax.shard_map(
        local,
        mesh=mesh,
        in_specs=placed,
        out_specs=(P("seq", "res", None), P(None, "res", "seq"), P(), P(), P(), P(), P()),
        check_vma=False,
    )
```

```python
import functools
import jax
import jax.numpy as jnp
from jax import lax
from jax.experimental import pallas as pl
from jax.experimental.pallas import tpu as pltpu
from jax.sharding import PartitionSpec as P

C = 64
H = 8
DH = 8
L = 2
PAIRS = 4
W = 128
EPSILON = 1e-05
MASKED = 1000000000.0
F32 = jnp.float32
BF16 = jnp.bfloat16
MESH = pl.DeviceIdType.MESH
NN = (((1,), (0,)), ((), ()))
NT = (((1,), (1,)), ((), ()))
TN = (((0,), (0,)), ((), ()))


def dot(a, b, dims=NN):
    return lax.dot_general(
        a, b, dims, precision=lax.Precision.HIGHEST, preferred_element_type=F32
    )


def dot1(a, b, dims=NN):
    return lax.dot_general(a, b, dims, preferred_element_type=F32)


def split2(a):
    high = a.astype(BF16)
    return high, (a - high.astype(F32)).astype(BF16)


def split3(a):
    high = a.astype(BF16)
    rest = a - high.astype(F32)
    middle = rest.astype(BF16)
    return high, middle, (rest - middle.astype(F32)).astype(BF16)


def dot3(a, b, dims=NN):
    ah, al = split2(a)
    bh, bl = split2(b)
    return dot1(ah, bh, dims) + (dot1(ah, bl, dims) + dot1(al, bh, dims))


def iota(shape, axis):
    return lax.broadcasted_iota(jnp.int32, shape, axis)


def ones_where(condition):
    return jnp.where(condition, 1.0, 0.0).astype(F32)


def twice(row):
    return jnp.concatenate([row, row], axis=1)


def fold(row):
    return row + jnp.concatenate([row[:, C:], row[:, :C]], axis=1)


def block_diagonal(weights):
    zero = jnp.zeros_like(weights)
    return jnp.concatenate(
        [jnp.concatenate([weights, zero], axis=1), jnp.concatenate([zero, weights], axis=1)], axis=0
    )


def diagonal_sum(full):
    return full[:C, :C] + full[C:, C:]


def kernel(
    sizes,
    align_hbm,
    cot_hbm,
    bias_hbm,
    gains_hbm,
    rowp_hbm,
    rowo_hbm,
    colp_hbm,
    colo_hbm,
    rmask_hbm,
    smask_hbm,
    galign_ref,
    gbias_ref,
    ggains_ref,
    growp_ref,
    growo_ref,
    gcolp_ref,
    gcolo_ref,
    xall,
    gsend,
    grecv,
    msend,
    mrecv,
    bsend,
    brecv,
    bias_t,
    exps,
    bias_s,
    core_r,
    x_s,
    x_r,
    y_s,
    y_r,
    zr_s,
    zr_r,
    pc_s,
    pc_r,
    pr_s,
    pr_r,
    t_s,
    t_r,
    o_r,
    align_ref,
    cot_ref,
    bias_ref,
    gains_ref,
    rowp_ref,
    rowo_ref,
    colp_ref,
    colo_ref,
    rmask_ref,
    smask_ref,
    send_sem,
    recv_sem,
    bias_send,
    bias_recv,
    load_sem,
    gather_send,
    gather_recv,
):
    ny, nx, nz = sizes
    ns = ny * nx * 2
    res = ns
    keys = nz * res
    wide = 4 * res
    half = 2 * res
    block = keys // ns
    me = lax.axis_index("seq")
    mz = lax.axis_index("res")
    core = lax.rem(me, 2)
    mx = lax.rem(me // 2, nx)
    my = me // (2 * nx)
    scaling = DH ** (-0.5)

    sources = (
        align_hbm,
        rmask_hbm,
        smask_hbm,
        cot_hbm,
        gains_hbm,
        rowp_hbm,
        rowo_hbm,
        bias_hbm,
        colp_hbm,
        colo_hbm,
    )
    targets = (
        align_ref,
        rmask_ref,
        smask_ref,
        cot_ref,
        gains_ref,
        rowp_ref,
        rowo_ref,
        bias_ref,
        colp_ref,
        colo_ref,
    )
    loads = [
        pltpu.make_async_copy(source, target, load_sem.at[i])
        for i, (source, target) in enumerate(zip(sources, targets))
    ]
    for load in loads:
        load.start()

    barrier = pltpu.get_barrier_semaphore()

    def greet_seq(i, carry):
        pl.semaphore_signal(
            barrier, inc=1, device_id=(lax.rem(me + i, ns), mz), device_id_type=MESH
        )
        return carry

    def greet_res(i, carry):
        pl.semaphore_signal(
            barrier, inc=1, device_id=(me, lax.rem(mz + i, nz)), device_id_type=MESH
        )
        return carry

    lax.fori_loop(1, nz, greet_res, 0)
    lax.fori_loop(1, ns, greet_seq, 0)

    def to_seq(source, target, which):
        def one(i, carry):
            j = lax.rem(me + i, ns)
            pltpu.make_async_remote_copy(
                src_ref=source(j),
                dst_ref=target.at[me],
                send_sem=send_sem.at[which],
                recv_sem=recv_sem.at[which],
                device_id=(j, mz),
                device_id_type=MESH,
            ).start()
            return carry

        lax.fori_loop(ns // 4, ns, one, 0)
        lax.fori_loop(1, ns // 4, one, 0)

    def to_res(source, target, which):
        def one(i, carry):
            j = lax.rem(mz + i, nz)
            pltpu.make_async_remote_copy(
                src_ref=source(j),
                dst_ref=target.at[mz],
                send_sem=send_sem.at[which],
                recv_sem=recv_sem.at[which],
                device_id=(me, j),
                device_id_type=MESH,
            ).start()
            return carry

        lax.fori_loop(1, nz, one, 0)

    def wait(ref, semaphore):
        pltpu.make_async_copy(ref, ref, semaphore).wait()

    def wait_all(buffer, which, count):
        part = buffer.at[pl.ds(0, count - 1)]
        wait(part, recv_sem.at[which])
        wait(part, send_sem.at[which])

    def keep(source, target, at):
        target[pl.ds(at, 1)] = source[pl.ds(at, 1)]

    ring = (3, nz - 3, 2, nz - 2, 1, nz - 1)
    cut = (res + 8) // 16 * 8

    def gather_copy(step):
        return pltpu.make_async_remote_copy(
            src_ref=xall.at[mz],
            dst_ref=xall.at[mz],
            send_sem=gather_send.at[step],
            recv_sem=gather_recv.at[step],
            device_id=(me, lax.rem(mz + step, nz)),
            device_id_type=MESH,
        )

    def gather_relay(step, rows, semaphore):
        part = xall.at[lax.rem(mz + nz - step, nz), rows]
        return pltpu.make_async_remote_copy(
            src_ref=part,
            dst_ref=part,
            send_sem=gather_send.at[semaphore],
            recv_sem=gather_recv.at[semaphore],
            device_id=(me, lax.rem(mz + (nz // 2 - step) + nz, nz)),
            device_id_type=MESH,
        )

    relays = ((3, pl.ds(0, cut), 0), (nz - 3, pl.ds(cut, res + 8 - cut), 4))

    def gather_start():
        if nz != 8:
            to_res(lambda j: xall.at[mz], xall, 0)
            return
        for step in ring:
            gather_copy(step).start()

    def gather_pass_on():
        if nz != 8:
            return
        for step, rows, semaphore in relays:
            gather_copy(step).wait_recv()
            gather_relay(step, rows, semaphore).start()

    def gather_wait():
        if nz != 8:
            wait_all(xall, 0, nz)
            return
        for step in ring[2:]:
            gather_copy(step).wait_recv()
        for relay in relays:
            gather_relay(*relay).wait_recv()

    def gather_finish():
        if nz != 8:
            return
        for step in ring:
            gather_copy(step).wait_send()
        for relay in relays:
            gather_relay(*relay).wait_send()

    for load in loads[:4]:
        load.wait()
    align = align_ref[...].astype(F32)
    initial = jnp.concatenate([align[0], align[1]], axis=1)
    cot = cot_ref[...].astype(F32)
    top_local = jnp.concatenate([cot[0], cot[1]], axis=1)
    averaging = ones_where(iota((W, W), 0) // C == iota((W, W), 1) // C) * (1.0 / C)

    def layer_norm(values):
        centred = values - dot(values, averaging)
        spread = dot(centred * centred, averaging)
        inverse = lax.rsqrt(spread + EPSILON)
        return centred * inverse, inverse

    def layer_norm_back(grad_normed, gain, hat, inverse):
        scaled = grad_normed * gain
        rows = scaled.shape[0]
        means = dot(jnp.concatenate([scaled, scaled * hat], axis=0), averaging)
        return inverse * (scaled - means[:rows] - hat * means[rows:])

    hat_local, inverse_local = layer_norm(initial)
    xall[mz, 0:res, :] = hat_local
    xall[mz, res : res + 8, :] = jnp.broadcast_to(
        jnp.concatenate([rmask_ref[...].astype(F32), jnp.zeros((1, W - res), F32)], axis=1), (8, W)
    )
    present_pair = smask_ref[...].astype(F32)
    present_row = jnp.concatenate(
        [jnp.broadcast_to(present_pair[:, i : i + 1], (1, C)) for i in range(L)], axis=1
    )
    gsend[:, 0, 0:W] = top_local
    gsend[:, 0, W : 2 * W] = jnp.broadcast_to(present_row, (res, W))

    pl.semaphore_wait(barrier, ns + nz - 2)
    gather_start()
    to_seq(lambda j: gsend.at[j], grecv, 1)
    keep(gsend, grecv, me)

    for load in loads[4:]:
        load.wait()
    gains = gains_ref[...]
    gain_row = twice(gains[0:1])
    gain_col = twice(gains[1:2])

    lane = iota((C, W), 1)
    column = (lane // 32) * 16 + lane % 16
    chosen = [
        ones_where((iota((C, W), 0) == column) & ((lane // 16) % 2 == s)) for s in range(L)
    ]

    def spread_columns(weights):
        return jnp.concatenate([dot(weights, chosen[0]), dot(weights, chosen[1])], axis=0)

    def gather_columns(full):
        return dot(full[:C], chosen[0], NT) + dot(full[C:], chosen[1], NT)

    rowp = rowp_ref[...]
    query_w = spread_columns(rowp[:, 0:C])
    key_w = spread_columns(rowp[:, C : 2 * C])
    value_w = spread_columns(rowp[:, 2 * C : 3 * C])
    gate_w = spread_columns(rowp[:, 3 * C :])
    rowo = rowo_ref[...]
    out_w = jnp.concatenate([dot(chosen[0], rowo, TN), dot(chosen[1], rowo, TN)], axis=1)
    memory_w = jnp.concatenate([key_w, value_w], axis=1)

    normed_local = hat_local * gain_row
    queries = dot(normed_local, query_w) * scaling
    gate_row = jax.nn.sigmoid(dot(normed_local, gate_w))

    gather_pass_on()
    for p in range(PAIRS):
        pair = bias_ref[2 * p : 2 * p + 2].astype(F32).reshape(half, keys)
        bias_t[p] = pair.T

    match = iota((W, wide), 0) // DH - iota((W, wide), 1) // res

    def heads_apart(rows):
        flat = rows.T
        flat = jnp.concatenate([flat, flat, flat, flat], axis=1)
        return [jnp.where(match == 4 * p, flat, 0.0) for p in range(PAIRS)]

    queries_apart = heads_apart(queries)
    query_terms = []
    for p in range(PAIRS):
        q1, q2, q3 = split3(queries_apart[p])
        query_terms.append(
            (
                jnp.concatenate([q1, q1], axis=0),
                jnp.concatenate([q2, q2], axis=0),
                jnp.concatenate([q3, q1], axis=0),
            )
        )

    mine = ones_where(iota((32, wide), 0) // DH == iota((32, wide), 1) // res)

    def heads_together(apart):
        kept = apart * mine
        both = kept[:, :half] + kept[:, half:]
        return both[:, :res] + both[:, res:]

    identity = ones_where(iota((C, C), 0) == iota((C, C), 1))
    colp = colp_ref[...]
    colo = colo_ref[...]
    entry = iota((C + 2 * DH + C, C), 0)
    entry_lane = iota((C + 2 * DH + C, C), 1)
    key_col_w = block_diagonal(dot(colp, ones_where(entry == C + entry_lane % DH)))
    value_col_w = block_diagonal(dot(colp, ones_where(entry == C + DH + entry_lane % DH)))
    gate_col_w = block_diagonal(dot(colp, ones_where(entry == C + 2 * DH + entry_lane)))
    query_col_w = block_diagonal(colp[:, 0:C])
    out_col_w = block_diagonal(colo)
    column_w = jnp.concatenate([key_col_w, value_col_w, gate_col_w], axis=1)
    head_sum = ones_where(iota((W, W), 0) // DH == iota((W, W), 1) // DH)

    gather_wait()
    hat_all = xall[:, 0:res, :].reshape(keys, W)
    normed_all = hat_all * gain_row
    memory = dot(normed_all, memory_w)
    key_rows = memory[:, :W]
    value_rows = memory[:, W:]
    value_flat = value_rows.T
    mask_flat = jnp.concatenate([xall[z, res : res + 8, :] for z in range(nz)], axis=0).T
    key_bias = jnp.concatenate(
        [MASKED * (mask_flat[:res, 8 * z : 8 * z + 1] - 1.0) for z in range(nz)], axis=0
    )
    k1, k2, k3 = split3(key_rows)
    k12 = jnp.concatenate([k1, k2], axis=1)
    k13 = jnp.concatenate([k1, k3], axis=1)
    value_high, value_low = split2(value_flat)

    totals = []
    mixed = []
    for p in range(PAIRS):
        terms = query_terms[p]
        scores = dot1(k12, terms[0]) + (dot1(k12, terms[1]) + dot1(k13, terms[2]))
        scores = scores + twice(bias_t[p]) + key_bias
        peak = jnp.max(scores, axis=0, keepdims=True)
        exponent = jnp.exp(scores - peak)
        exps[p] = exponent
        inverse_total = 1.0 / jnp.sum(exponent, axis=0, keepdims=True)
        totals.append(inverse_total)
        eh, el = split2(exponent)
        vh = value_high[32 * p : 32 * p + 32]
        vl = value_low[32 * p : 32 * p + 32]
        apart = dot1(vh, eh) + (dot1(vl, eh) + dot1(vh, el))
        mixed.append(heads_together(apart * inverse_total))
    mixture = jnp.concatenate(mixed, axis=0).T
    gated = gate_row * mixture
    middle = initial + dot(gated, out_w)
    msend[:, 0, :] = middle
    to_seq(lambda j: msend.at[j], mrecv, 2)
    keep(msend, mrecv, me)

    wait_all(grecv, 1, ns)
    top = grecv[:, 0, 0:W]
    present = grecv[:, 0, W : 2 * W]
    counted = jnp.sum(fold(jnp.sum(present, axis=0, keepdims=True)), axis=1, keepdims=True) * (
        1.0 / W
    )
    inverse_count = 1.0 / counted
    grad_gated_col = dot(top, out_col_w, NT)

    wait_all(mrecv, 2, ns)
    hat_col, inverse_col = layer_norm(mrecv[:, 0, :])
    normed_col = hat_col * gain_col
    mean_normed = fold(jnp.sum(present * normed_col, axis=0, keepdims=True)) * inverse_count
    queries_col = dot(mean_normed, query_col_w) * scaling
    projected = dot(normed_col, column_w)
    key_col = projected[:, 0:W]
    value_col = projected[:, W : 2 * W]
    gate_col = jax.nn.sigmoid(projected[:, 2 * W :])
    scores_col = dot(key_col * queries_col, head_sum) + MASKED * (present - 1.0)
    peak_row = jnp.max(scores_col, axis=0, keepdims=True)
    peak_row = jnp.maximum(peak_row, jnp.concatenate([peak_row[:, C:], peak_row[:, :C]], axis=1))
    exp_col = jnp.exp(scores_col - peak_row)
    weights_col = exp_col * (1.0 / fold(jnp.sum(exp_col, axis=0, keepdims=True)))
    mixture_col = fold(jnp.sum(weights_col * value_col, axis=0, keepdims=True))
    grad_mixture_col = fold(jnp.sum(gate_col * grad_gated_col, axis=0, keepdims=True))
    grad_gate_col = grad_gated_col * mixture_col * gate_col * (1.0 - gate_col)
    grad_weights_col = dot(value_col * grad_mixture_col, head_sum)
    inner_col = fold(jnp.sum(weights_col * grad_weights_col, axis=0, keepdims=True))
    grad_scores_col = weights_col * (grad_weights_col - inner_col)
    grad_query_col = fold(jnp.sum(grad_scores_col * key_col, axis=0, keepdims=True)) * scaling
    grad_key_col = grad_scores_col * queries_col
    grad_value_col = weights_col * grad_mixture_col
    grad_mean = dot(grad_query_col, query_col_w, NT)
    grad_projected = jnp.concatenate([grad_key_col, grad_value_col, grad_gate_col], axis=1)
    grad_normed_col = present * inverse_count * grad_mean + dot(grad_projected, column_w, NT)
    grad_middle_col = top + layer_norm_back(grad_normed_col, gain_col, hat_col, inverse_col)
    bsend[:, 0, :] = grad_middle_col
    to_seq(lambda j: bsend.at[j], brecv, 3)
    keep(bsend, brecv, me)

    pack_lane = iota((C, 2 * W), 1)
    pack_row = iota((C, 2 * W), 0)
    grad_full = dot(hat_col, grad_projected, TN)
    mean_hat = fold(jnp.sum(present * hat_col, axis=0, keepdims=True)) * inverse_count
    mean_column = jnp.sum(identity * mean_hat[:, :C], axis=1, keepdims=True)
    grad_col_parts = jnp.concatenate(
        [
            mean_column * grad_query_col[:, :C],
            diagonal_sum(grad_full[:, 0:W]),
            diagonal_sum(grad_full[:, W : 2 * W]),
            diagonal_sum(grad_full[:, 2 * W :]),
            diagonal_sum(dot(gate_col * mixture_col, top, TN)),
        ],
        axis=1,
    )
    placing = jnp.concatenate(
        [
            ones_where(pack_lane == pack_row),
            ones_where(pack_lane == C + pack_row % DH),
            ones_where(pack_lane == C + DH + pack_row % DH),
            ones_where(pack_lane == C + 2 * DH + pack_row),
            ones_where(pack_lane == 2 * C + 2 * DH + pack_row),
        ],
        axis=0,
    )
    pack = dot(grad_col_parts, placing)
    pc_s[...] = pack.reshape(ns, C // ns, 2 * W)
    to_seq(lambda j: pc_s.at[j], pc_r, 4)
    keep(pc_s, pc_r, me)

    key_flat = key_rows.T
    key_high, key_low = split2(key_flat)
    v1, v2 = split2(value_rows)
    v12 = jnp.concatenate([v1, v2], axis=1)

    wait_all(brecv, 3, ns)
    grad_middle = brecv[:, 0, :]
    grad_gated = dot(grad_middle, out_w, NT)
    grad_gate = grad_gated * mixture * gate_row * (1.0 - gate_row)
    grads_apart = heads_apart(grad_gated * gate_row)
    grad_out_w = dot(gated, grad_middle, TN)
    grad_rowo = dot(chosen[0], grad_out_w[:, :C]) + dot(chosen[1], grad_out_w[:, C:])

    def bias_core(p):
        return pltpu.make_async_remote_copy(
            src_ref=bias_s.at[p, :, :, 1 - core],
            dst_ref=core_r.at[p],
            send_sem=bias_send.at[0, p],
            recv_sem=bias_recv.at[0, p],
            device_id=(me + 1 - 2 * core, mz),
            device_id_type=MESH,
        )

    def bias_to_x(p):
        bias_core(p).wait()
        x_s[p] = jnp.swapaxes(bias_s[p, :, :, core] + core_r[p], 0, 1)

        def one(i, carry):
            j = lax.rem(mx + i, nx)
            pltpu.make_async_remote_copy(
                src_ref=x_s.at[p, j],
                dst_ref=x_r.at[p, mx],
                send_sem=bias_send.at[1, p],
                recv_sem=bias_recv.at[1, p],
                device_id=((my * nx + j) * 2 + core, mz),
                device_id_type=MESH,
            ).start()
            return carry

        lax.fori_loop(1, nx, one, 0)
        x_r[p, pl.ds(mx, 1)] = x_s[p, pl.ds(mx, 1)]

    def bias_to_y(p):
        part = x_r.at[p, pl.ds(0, nx - 1)]
        wait(part, bias_recv.at[1, p])
        wait(part, bias_send.at[1, p])
        y_s[p] = sum([x_r[p, i] for i in range(1, nx)], x_r[p, 0])

        def one(i, carry):
            j = lax.rem(my + i, ny)
            pltpu.make_async_remote_copy(
                src_ref=y_s.at[p, j],
                dst_ref=y_r.at[p, my],
                send_sem=bias_send.at[2, p],
                recv_sem=bias_recv.at[2, p],
                device_id=((j * nx + mx) * 2 + core, mz),
                device_id_type=MESH,
            ).start()
            return carry

        lax.fori_loop(1, ny, one, 0)
        y_r[p, pl.ds(my, 1)] = y_s[p, pl.ds(my, 1)]

    def bias_done(p):
        part = y_r.at[p, pl.ds(0, ny - 1)]
        wait(part, bias_recv.at[2, p])
        wait(part, bias_send.at[2, p])
        total = sum([y_r[p, i] for i in range(1, ny)], y_r[p, 0])
        gbias_ref[2 * p] = total[:, :res]
        gbias_ref[2 * p + 1] = total[:, res:]

    grad_keys = jnp.zeros((keys, W), F32)
    grad_values = jnp.zeros((keys, W), F32)
    grad_queries = []
    for p in range(PAIRS):
        gh, gl = split2(grads_apart[p])
        grad_weights = dot1(v12, jnp.concatenate([gh, gh], axis=0)) + dot1(v1, gl)
        weights = exps[p] * totals[p]
        inner = jnp.sum(weights * grad_weights, axis=0, keepdims=True)
        grad_scores = weights * (grad_weights - inner)
        bias_s[p] = (grad_scores[:, :half] + grad_scores[:, half:]).reshape(
            ny, nx, 2, block, half
        )
        bias_core(p).start()
        sh, sl = split2(grad_scores)
        wh, wl = split2(weights)
        q1, q2 = split2(queries_apart[p])
        grad_keys = grad_keys + (dot1(sh, q1, NT) + (dot1(sh, q2, NT) + dot1(sl, q1, NT)))
        grad_values = grad_values + (dot1(wh, gh, NT) + (dot1(wh, gl, NT) + dot1(wl, gh, NT)))
        kh = key_high[32 * p : 32 * p + 32]
        kl = key_low[32 * p : 32 * p + 32]
        grad_queries.append(
            heads_together(dot1(kh, sh) + (dot1(kl, sh) + dot1(kh, sl)))
        )
        if p >= 1:
            bias_to_x(p - 1)

    grad_memory = jnp.concatenate([grad_keys, grad_values], axis=1)
    grad_query = jnp.concatenate(grad_queries, axis=0).T * scaling
    own_grads = jnp.concatenate([grad_query, grad_gate], axis=1)
    grad_memory_w = dot3(hat_all, grad_memory, TN)
    grad_own_w = dot(hat_local, own_grads, TN)
    pack_row_part = jnp.concatenate(
        [
            gather_columns(grad_own_w[:, :W]),
            gather_columns(grad_memory_w[:, :W]),
            gather_columns(grad_memory_w[:, W:]),
            gather_columns(grad_own_w[:, W:]),
            grad_rowo,
            jnp.zeros((C, C), F32),
        ],
        axis=1,
    )
    pr_s[...] = pack_row_part.reshape(ns, C // ns, 3 * W)
    to_seq(lambda j: pr_s.at[j], pr_r, 6)
    keep(pr_s, pr_r, me)

    zr_s[...] = dot3(grad_memory, memory_w, NT).reshape(nz, res, W)
    to_res(lambda j: zr_s.at[j], zr_r, 5)
    keep(zr_s, zr_r, mz)
    bias_to_x(PAIRS - 1)
    own_normed_grad = dot(own_grads, jnp.concatenate([query_w, gate_w], axis=1), NT)
    for p in range(PAIRS):
        bias_to_y(p)

    wait_all(pc_r, 4, ns)
    wait_all(pr_r, 6, ns)
    t_s[...] = jnp.concatenate(
        [jnp.sum(pr_r[...], axis=0), jnp.sum(pc_r[...], axis=0)], axis=1
    )
    to_res(lambda j: t_s, t_r, 7)
    t_r[pl.ds(mz, 1)] = t_s[...][None]

    wait_all(zr_r, 5, nz)
    grad_normed_row = sum([zr_r[i] for i in range(1, nz)], zr_r[0]) + own_normed_grad
    grad_initial = layer_norm_back(grad_normed_row, gain_row, hat_local, inverse_local)
    grad_align = (grad_middle + grad_initial).astype(BF16)
    galign_ref[0] = grad_align[:, :C]
    galign_ref[1] = grad_align[:, C:]

    wait_all(t_r, 7, nz)
    o_r[me] = sum([t_r[i] for i in range(1, nz)], t_r[0])
    to_seq(lambda j: o_r.at[me], o_r, 8)
    for p in range(PAIRS):
        bias_done(p)
    gather_finish()
    gain_columns = [
        jnp.sum(identity * gains[i : i + 1], axis=1, keepdims=True) for i in range(2)
    ]
    wait_all(o_r, 8, ns)
    final = o_r[...].reshape(C, 5 * W)
    row_part = final[:, 0 : 4 * C]
    col_part = final[:, 3 * W : 3 * W + 2 * C + 2 * DH]
    growp_ref[...] = row_part * gain_columns[0]
    growo_ref[...] = final[:, 4 * C : 5 * C]
    gcolp_ref[...] = col_part * gain_columns[1]
    gcolo_ref[...] = final[:, 3 * W + 2 * C + 2 * DH : 3 * W + 3 * C + 2 * DH]
    for i, (part, weights) in enumerate(((row_part, rowp), (col_part, colp))):
        column_sum = jnp.sum(part * weights, axis=1, keepdims=True)
        ggains_ref[i : i + 1, :] = jnp.sum(identity * column_sum, axis=0, keepdims=True)


def store_all(*refs):
    count = (len(refs) - 1) // 2
    semaphores = refs[-1]
    copies = [
        pltpu.make_async_copy(refs[i], refs[count + i], semaphores.at[i]) for i in range(count)
    ]
    for copy in copies:
        copy.start()
    for copy in copies:
        copy.wait()


def finish(arrays):
    arrays = pl.pallas_call(
        store_all,
        out_shape=tuple(jax.ShapeDtypeStruct(a.shape, a.dtype) for a in arrays),
        in_specs=[pl.BlockSpec(memory_space=pltpu.VMEM)] * len(arrays),
        out_specs=(pl.BlockSpec(memory_space=pltpu.HBM),) * len(arrays),
        scratch_shapes=[pltpu.SemaphoreType.DMA((len(arrays),))],
    )(*arrays)
    return (arrays[0], jnp.swapaxes(arrays[1], 1, 2)) + tuple(arrays[2:])


def solution(mesh):
    seq_devices = mesh.shape["seq"]
    res_devices = mesh.shape["res"]
    nx = 4 if seq_devices == 64 else 2
    ny = seq_devices // (2 * nx)
    nz = res_devices
    res = seq_devices
    keys = nz * res
    block = keys // seq_devices
    half = 2 * res

    def local(
        alignment,
        cotangent,
        pair_bias,
        norm_gains,
        row_project,
        row_output,
        column_project,
        column_output,
        residue_mask,
        sequence_mask,
    ):
        vmem = pl.BlockSpec(memory_space=pltpu.VMEM)
        ns = seq_devices
        chunk = C // ns
        outs = pl.pallas_call(
            functools.partial(kernel, (ny, nx, nz)),
            out_shape=(
                jax.ShapeDtypeStruct((L, res, C), BF16),
                jax.ShapeDtypeStruct((H, block, res), F32),
                jax.ShapeDtypeStruct((2, C), F32),
                jax.ShapeDtypeStruct((C, 4 * C), F32),
                jax.ShapeDtypeStruct((C, C), F32),
                jax.ShapeDtypeStruct((C, 2 * C + 2 * DH), F32),
                jax.ShapeDtypeStruct((C, C), F32),
            ),
            in_specs=[pl.BlockSpec(memory_space=pltpu.HBM)] * 10,
            out_specs=(vmem,) * 7,
            scratch_shapes=[
                pltpu.VMEM((nz, res + 8, W), F32),
                pltpu.VMEM((ns, 1, 2 * W), F32),
                pltpu.VMEM((ns, 1, 2 * W), F32),
                pltpu.VMEM((ns, 1, W), F32),
                pltpu.VMEM((ns, 1, W), F32),
                pltpu.VMEM((ns, 1, W), F32),
                pltpu.VMEM((ns, 1, W), F32),
                pltpu.VMEM((PAIRS, keys, half), F32),
                pltpu.VMEM((PAIRS, keys, 2 * half), F32),
                pltpu.VMEM((PAIRS, ny, nx, 2, block, half), F32),
                pltpu.VMEM((PAIRS, ny, nx, block, half), F32),
                pltpu.VMEM((PAIRS, nx, ny, block, half), F32),
                pltpu.VMEM((PAIRS, nx, ny, block, half), F32),
                pltpu.VMEM((PAIRS, ny, block, half), F32),
                pltpu.VMEM((PAIRS, ny, block, half), F32),
                pltpu.VMEM((nz, res, W), F32),
                pltpu.VMEM((nz, res, W), F32),
                pltpu.VMEM((ns, chunk, 2 * W), F32),
                pltpu.VMEM((ns, chunk, 2 * W), F32),
                pltpu.VMEM((ns, chunk, 3 * W), F32),
                pltpu.VMEM((ns, chunk, 3 * W), F32),
                pltpu.VMEM((chunk, 5 * W), F32),
                pltpu.VMEM((nz, chunk, 5 * W), F32),
                pltpu.VMEM((ns, chunk, 5 * W), F32),
                pltpu.VMEM((L, res, C), BF16),
                pltpu.VMEM((L, res, C), BF16),
                pltpu.VMEM((H, res, keys), BF16),
                pltpu.VMEM((2, C), F32),
                pltpu.VMEM((C, 4 * C), F32),
                pltpu.VMEM((C, C), F32),
                pltpu.VMEM((C, 2 * C + 2 * DH), F32),
                pltpu.VMEM((C, C), F32),
                pltpu.VMEM((1, res), jnp.int32),
                pltpu.VMEM((1, L), jnp.int32),
                pltpu.SemaphoreType.DMA((9,)),
                pltpu.SemaphoreType.DMA((9,)),
                pltpu.SemaphoreType.DMA((3, PAIRS)),
                pltpu.SemaphoreType.DMA((3, PAIRS)),
                pltpu.SemaphoreType.DMA((10,)),
                pltpu.SemaphoreType.DMA((8,)),
                pltpu.SemaphoreType.DMA((8,)),
            ],
            compiler_params=pltpu.CompilerParams(
                collective_id=0, has_side_effects=True, vmem_limit_bytes=64 * 1024 * 1024
            ),
        )(
            alignment,
            cotangent,
            pair_bias,
            norm_gains,
            row_project,
            row_output,
            column_project,
            column_output,
            residue_mask[None],
            sequence_mask[None],
        )
        return finish(outs)

    placed = (
        P("seq", "res", None),
        P("seq", "res", None),
        P(None, "res", None),
        P(),
        P(),
        P(),
        P(),
        P(),
        P("res"),
        P("seq"),
    )
    return jax.shard_map(
        local,
        mesh=mesh,
        in_specs=placed,
        out_specs=(P("seq", "res", None), P(None, "res", "seq"), P(), P(), P(), P(), P()),
        check_vma=False,
    )
```

```python
import functools
import jax
import jax.numpy as jnp
from jax import lax
from jax.experimental import pallas as pl
from jax.experimental.pallas import tpu as pltpu
from jax.sharding import PartitionSpec as P

C = 64
H = 8
DH = 8
L = 2
PAIRS = 4
W = 128
EPSILON = 1e-05
MASKED = 1000000000.0
F32 = jnp.float32
BF16 = jnp.bfloat16
MESH = pl.DeviceIdType.MESH
NN = (((1,), (0,)), ((), ()))
NT = (((1,), (1,)), ((), ()))
TN = (((0,), (0,)), ((), ()))


def dot(a, b, dims=NN):
    return lax.dot_general(
        a, b, dims, precision=lax.Precision.HIGHEST, preferred_element_type=F32
    )


def dot1(a, b, dims=NN):
    return lax.dot_general(a, b, dims, preferred_element_type=F32)


def split2(a):
    high = a.astype(BF16)
    return high, (a - high.astype(F32)).astype(BF16)


def split3(a):
    high = a.astype(BF16)
    rest = a - high.astype(F32)
    middle = rest.astype(BF16)
    return high, middle, (rest - middle.astype(F32)).astype(BF16)


def dot3(a, b, dims=NN):
    ah, al = split2(a)
    bh, bl = split2(b)
    return dot1(ah, bh, dims) + (dot1(ah, bl, dims) + dot1(al, bh, dims))


def products(first, second):
    a1, a2, a3 = first
    b1, b2, b3 = second
    a12 = jnp.concatenate([a1, a2], axis=1)
    a13 = jnp.concatenate([a1, a3], axis=1)
    return dot1(a12, jnp.concatenate([b1, b1], axis=0)) + (
        dot1(a12, jnp.concatenate([b2, b2], axis=0)) + dot1(a13, jnp.concatenate([b3, b1], axis=0))
    )


def pick(values, ones, dims=NN):
    ones = ones.astype(BF16)
    axis = dims[0][1][0]
    return dot1(
        jnp.concatenate(split2(values), axis=1), jnp.concatenate([ones, ones], axis=axis), dims
    )


def outer3(left, right):
    lh, ll = left
    rh, rl = right
    both = dot1(lh, jnp.concatenate([rh, rl], axis=0), NT)
    count = rh.shape[0]
    return both[:, :count] + (both[:, count:] + dot1(ll, rh, NT))


def iota(shape, axis):
    return lax.broadcasted_iota(jnp.int32, shape, axis)


def ones_where(condition):
    return jnp.where(condition, 1.0, 0.0).astype(F32)


def twice(row):
    return jnp.concatenate([row, row], axis=1)


def fold(row):
    return row + jnp.concatenate([row[:, C:], row[:, :C]], axis=1)


def block_diagonal(weights):
    zero = jnp.zeros_like(weights)
    return jnp.concatenate(
        [jnp.concatenate([weights, zero], axis=1), jnp.concatenate([zero, weights], axis=1)], axis=0
    )


def diagonal_sum(full):
    return full[:C, :C] + full[C:, C:]


def kernel(
    sizes,
    align_hbm,
    cot_hbm,
    bias_hbm,
    gains_hbm,
    rowp_hbm,
    rowo_hbm,
    colp_hbm,
    colo_hbm,
    rmask_hbm,
    smask_hbm,
    galign_hbm,
    gbias_hbm,
    ggains_hbm,
    growp_hbm,
    growo_hbm,
    gcolp_hbm,
    gcolo_hbm,
    xall,
    gsend,
    grecv,
    msend,
    mrecv,
    bsend,
    brecv,
    bias_t,
    exps,
    bias_s,
    core_r,
    x_s,
    x_r,
    y_s,
    y_r,
    zr_s,
    zr_r,
    pc_s,
    pc_r,
    pr_s,
    pr_r,
    t_s,
    t_r,
    o_r,
    tc_s,
    tc_r,
    oc_r,
    align_ref,
    cot_ref,
    bias_ref,
    gains_ref,
    rowp_ref,
    rowo_ref,
    colp_ref,
    colo_ref,
    rmask_ref,
    smask_ref,
    send_sem,
    recv_sem,
    bias_send,
    bias_recv,
    load_sem,
    gather_send,
    gather_recv,
    galign_ref,
    gbias_ref,
    ggains_ref,
    growp_ref,
    growo_ref,
    gcolp_ref,
    gcolo_ref,
    store_sem,
):
    ny, nx, nz = sizes
    ns = ny * nx * 2
    res = ns
    keys = nz * res
    wide = 4 * res
    half = 2 * res
    block = keys // ns
    me = lax.axis_index("seq")
    mz = lax.axis_index("res")
    core = lax.rem(me, 2)
    mx = lax.rem(me // 2, nx)
    my = me // (2 * nx)
    scaling = DH ** (-0.5)

    sources = (
        align_hbm,
        rmask_hbm,
        smask_hbm,
        cot_hbm,
        gains_hbm,
        rowp_hbm,
        rowo_hbm,
        bias_hbm,
        colp_hbm,
        colo_hbm,
    )
    targets = (
        align_ref,
        rmask_ref,
        smask_ref,
        cot_ref,
        gains_ref,
        rowp_ref,
        rowo_ref,
        bias_ref,
        colp_ref,
        colo_ref,
    )
    loads = [
        pltpu.make_async_copy(source, target, load_sem.at[i])
        for i, (source, target) in enumerate(zip(sources, targets))
    ]
    for load in loads:
        load.start()

    barrier = pltpu.get_barrier_semaphore()

    def greet_seq(i, carry):
        pl.semaphore_signal(
            barrier, inc=1, device_id=(lax.rem(me + i, ns), mz), device_id_type=MESH
        )
        return carry

    def greet_res(i, carry):
        pl.semaphore_signal(
            barrier, inc=1, device_id=(me, lax.rem(mz + i, nz)), device_id_type=MESH
        )
        return carry

    lax.fori_loop(1, nz, greet_res, 0)
    lax.fori_loop(ns // 4, ns, greet_seq, 0)
    lax.fori_loop(1, ns // 4, greet_seq, 0)

    stores = [
        pltpu.make_async_copy(source, target, store_sem.at[i])
        for i, (source, target) in enumerate(
            (
                (galign_ref, galign_hbm),
                (gbias_ref, gbias_hbm),
                (ggains_ref, ggains_hbm),
                (growp_ref, growp_hbm),
                (growo_ref, growo_hbm),
                (gcolp_ref, gcolp_hbm),
                (gcolo_ref, gcolo_hbm),
            )
        )
    ]

    def to_seq(source, target, which):
        def one(i, carry):
            j = lax.rem(me + i, ns)
            pltpu.make_async_remote_copy(
                src_ref=source(j),
                dst_ref=target.at[me],
                send_sem=send_sem.at[which],
                recv_sem=recv_sem.at[which],
                device_id=(j, mz),
                device_id_type=MESH,
            ).start()
            return carry

        lax.fori_loop(ns // 4, ns, one, 0)
        lax.fori_loop(1, ns // 4, one, 0)

    def to_res(source, target, which):
        def one(i, carry):
            j = lax.rem(mz + i, nz)
            pltpu.make_async_remote_copy(
                src_ref=source(j),
                dst_ref=target.at[mz],
                send_sem=send_sem.at[which],
                recv_sem=recv_sem.at[which],
                device_id=(me, j),
                device_id_type=MESH,
            ).start()
            return carry

        lax.fori_loop(1, nz, one, 0)

    def wait(ref, semaphore):
        pltpu.make_async_copy(ref, ref, semaphore).wait()

    def wait_all(buffer, which, count):
        part = buffer.at[pl.ds(0, count - 1)]
        wait(part, recv_sem.at[which])
        wait(part, send_sem.at[which])

    def keep(source, target, at):
        target[pl.ds(at, 1)] = source[pl.ds(at, 1)]

    ring = (3, nz - 3, 2, nz - 2, 1, nz - 1)
    cut = (res + 8) // 16 * 8

    def gather_copy(step):
        return pltpu.make_async_remote_copy(
            src_ref=xall.at[mz],
            dst_ref=xall.at[mz],
            send_sem=gather_send.at[step],
            recv_sem=gather_recv.at[step],
            device_id=(me, lax.rem(mz + step, nz)),
            device_id_type=MESH,
        )

    def gather_relay(step, rows, semaphore):
        part = xall.at[lax.rem(mz + nz - step, nz), rows]
        return pltpu.make_async_remote_copy(
            src_ref=part,
            dst_ref=part,
            send_sem=gather_send.at[semaphore],
            recv_sem=gather_recv.at[semaphore],
            device_id=(me, lax.rem(mz + (nz // 2 - step) + nz, nz)),
            device_id_type=MESH,
        )

    relays = ((3, pl.ds(0, cut), 0), (nz - 3, pl.ds(cut, res + 8 - cut), 4))

    def gather_start():
        if nz != 8:
            to_res(lambda j: xall.at[mz], xall, 0)
            return
        for step in ring:
            gather_copy(step).start()

    def gather_pass_on():
        if nz != 8:
            return
        for step, rows, semaphore in relays:
            gather_copy(step).wait_recv()
            gather_relay(step, rows, semaphore).start()

    def gather_wait():
        if nz != 8:
            wait_all(xall, 0, nz)
            return
        for step in ring[2:]:
            gather_copy(step).wait_recv()
        for relay in relays:
            gather_relay(*relay).wait_recv()

    def gather_finish():
        if nz != 8:
            return
        for step in ring:
            gather_copy(step).wait_send()
        for relay in relays:
            gather_relay(*relay).wait_send()

    for load in loads[:4]:
        load.wait()
    align = align_ref[...].astype(F32)
    initial = jnp.concatenate([align[0], align[1]], axis=1)
    cot = cot_ref[...].astype(F32)
    top_local = jnp.concatenate([cot[0], cot[1]], axis=1)
    averaging = ones_where(iota((W, W), 0) // C == iota((W, W), 1) // C) * (1.0 / C)

    def layer_norm(values):
        centred = values - dot(values, averaging)
        spread = dot(centred * centred, averaging)
        inverse = lax.rsqrt(spread + EPSILON)
        return centred * inverse, inverse

    def layer_norm_back(grad_normed, gain, hat, inverse):
        scaled = grad_normed * gain
        rows = scaled.shape[0]
        means = dot(jnp.concatenate([scaled, scaled * hat], axis=0), averaging)
        return inverse * (scaled - means[:rows] - hat * means[rows:])

    hat_local, inverse_local = layer_norm(initial)
    xall[mz, 0:res, :] = hat_local
    xall[mz, res : res + 8, :] = jnp.broadcast_to(
        jnp.concatenate([rmask_ref[...].astype(F32), jnp.zeros((1, W - res), F32)], axis=1), (8, W)
    )
    present_pair = smask_ref[...].astype(F32)
    present_row = jnp.concatenate(
        [jnp.broadcast_to(present_pair[:, i : i + 1], (1, C)) for i in range(L)], axis=1
    )
    gsend[:, 0, 0:W] = top_local
    gsend[:, 0, W : 2 * W] = jnp.broadcast_to(present_row, (res, W))

    pl.semaphore_wait(barrier, ns + nz - 2)
    gather_start()
    to_seq(lambda j: gsend.at[j], grecv, 1)
    keep(gsend, grecv, me)

    for load in loads[4:]:
        load.wait()
    gains = gains_ref[...]
    gain_row = twice(gains[0:1])
    gain_col = twice(gains[1:2])

    lane = iota((C, W), 1)
    column = (lane // 32) * 16 + lane % 16
    chosen = [
        ones_where((iota((C, W), 0) == column) & ((lane // 16) % 2 == s)) for s in range(L)
    ]

    def spread_columns(weights):
        return jnp.concatenate([dot(weights, chosen[0]), dot(weights, chosen[1])], axis=0)

    rowp = rowp_ref[...]
    query_w = spread_columns(rowp[:, 0:C])
    key_w = spread_columns(rowp[:, C : 2 * C])
    value_w = spread_columns(rowp[:, 2 * C : 3 * C])
    gate_w = spread_columns(rowp[:, 3 * C :])
    rowo = rowo_ref[...]
    out_w = jnp.concatenate([dot(chosen[0], rowo, TN), dot(chosen[1], rowo, TN)], axis=1)
    memory_w = jnp.concatenate([key_w, value_w], axis=1)

    normed_local = hat_local * gain_row
    queries = dot(normed_local, query_w) * scaling
    gate_row = jax.nn.sigmoid(dot(normed_local, gate_w))

    gather_pass_on()
    for p in range(PAIRS):
        pair = bias_ref[2 * p : 2 * p + 2].astype(F32).reshape(half, keys)
        bias_t[p] = pair.T

    match = iota((W, wide), 0) // DH - iota((W, wide), 1) // res

    def heads_apart(rows):
        flat = rows.T
        flat = jnp.concatenate([flat, flat, flat, flat], axis=1)
        return [jnp.where(match == 4 * p, flat, 0.0) for p in range(PAIRS)]

    queries_apart = heads_apart(queries)
    query_terms = [split3(apart) for apart in queries_apart]

    mine = ones_where(iota((32, wide), 0) // DH == iota((32, wide), 1) // res)

    def heads_together(apart):
        kept = apart * mine
        both = kept[:, :half] + kept[:, half:]
        return both[:, :res] + both[:, res:]

    identity = ones_where(iota((C, C), 0) == iota((C, C), 1))
    colp = colp_ref[...]
    colo = colo_ref[...]
    entry = iota((C + 2 * DH + C, C), 0)
    entry_lane = iota((C + 2 * DH + C, C), 1)
    key_col_w = block_diagonal(dot(colp, ones_where(entry == C + entry_lane % DH)))
    value_col_w = block_diagonal(dot(colp, ones_where(entry == C + DH + entry_lane % DH)))
    gate_col_w = block_diagonal(dot(colp, ones_where(entry == C + 2 * DH + entry_lane)))
    query_col_w = block_diagonal(colp[:, 0:C])
    out_col_w = block_diagonal(colo)
    column_w = jnp.concatenate([key_col_w, value_col_w, gate_col_w], axis=1)
    head_sum = ones_where(iota((W, W), 0) // DH == iota((W, W), 1) // DH)

    gather_wait()
    hat_all = xall[:, 0:res, :].reshape(keys, W)
    normed_all = hat_all * gain_row
    memory = products(split3(normed_all), split3(memory_w))
    key_rows = memory[:, :W]
    value_rows = memory[:, W:]
    value_flat = value_rows.T
    mask_flat = jnp.concatenate([xall[z, res : res + 8, :] for z in range(nz)], axis=0).T
    key_bias = jnp.concatenate(
        [MASKED * (mask_flat[:res, 8 * z : 8 * z + 1] - 1.0) for z in range(nz)], axis=0
    )
    key_terms = split3(key_rows)
    value_high, value_low = split2(value_flat)

    totals = []
    mixed = []
    for p in range(PAIRS):
        scores = products(key_terms, query_terms[p])
        scores = scores + twice(bias_t[p]) + key_bias
        peak = jnp.max(scores, axis=0, keepdims=True)
        exponent = jnp.exp(scores - peak)
        exps[p] = exponent
        inverse_total = 1.0 / jnp.sum(exponent, axis=0, keepdims=True)
        totals.append(inverse_total)
        eh, el = split2(exponent)
        vh = value_high[32 * p : 32 * p + 32]
        vl = value_low[32 * p : 32 * p + 32]
        apart = dot1(vh, eh) + (dot1(vl, eh) + dot1(vh, el))
        mixed.append(heads_together(apart * inverse_total))
    mixture = jnp.concatenate(mixed, axis=0).T
    gated = gate_row * mixture
    middle = initial + dot(gated, out_w)
    msend[:, 0, :] = middle
    to_seq(lambda j: msend.at[j], mrecv, 2)
    keep(msend, mrecv, me)

    key_flat = key_rows.T
    key_high, key_low = split2(key_flat)
    v1, v2 = split2(value_rows)
    hat_high, hat_low = split2(hat_all.T)
    v12 = jnp.concatenate([v1, v2], axis=1)

    wait_all(grecv, 1, ns)
    top = grecv[:, 0, 0:W]
    present = grecv[:, 0, W : 2 * W]
    counted = jnp.sum(fold(jnp.sum(present, axis=0, keepdims=True)), axis=1, keepdims=True) * (
        1.0 / W
    )
    inverse_count = 1.0 / counted
    grad_gated_col = dot(top, out_col_w, NT)

    wait_all(mrecv, 2, ns)
    hat_col, inverse_col = layer_norm(mrecv[:, 0, :])
    normed_col = hat_col * gain_col
    mean_normed = fold(jnp.sum(present * normed_col, axis=0, keepdims=True)) * inverse_count
    queries_col = dot(mean_normed, query_col_w) * scaling
    projected = dot(normed_col, column_w)
    key_col = projected[:, 0:W]
    value_col = projected[:, W : 2 * W]
    gate_col = jax.nn.sigmoid(projected[:, 2 * W :])
    scores_col = dot(key_col * queries_col, head_sum) + MASKED * (present - 1.0)
    peak_row = jnp.max(scores_col, axis=0, keepdims=True)
    peak_row = jnp.maximum(peak_row, jnp.concatenate([peak_row[:, C:], peak_row[:, :C]], axis=1))
    exp_col = jnp.exp(scores_col - peak_row)
    weights_col = exp_col * (1.0 / fold(jnp.sum(exp_col, axis=0, keepdims=True)))
    mixture_col = fold(jnp.sum(weights_col * value_col, axis=0, keepdims=True))
    grad_mixture_col = fold(jnp.sum(gate_col * grad_gated_col, axis=0, keepdims=True))
    grad_gate_col = grad_gated_col * mixture_col * gate_col * (1.0 - gate_col)
    grad_weights_col = dot(value_col * grad_mixture_col, head_sum)
    inner_col = fold(jnp.sum(weights_col * grad_weights_col, axis=0, keepdims=True))
    grad_scores_col = weights_col * (grad_weights_col - inner_col)
    grad_query_col = fold(jnp.sum(grad_scores_col * key_col, axis=0, keepdims=True)) * scaling
    grad_key_col = grad_scores_col * queries_col
    grad_value_col = weights_col * grad_mixture_col
    grad_mean = dot(grad_query_col, query_col_w, NT)
    grad_projected = jnp.concatenate([grad_key_col, grad_value_col, grad_gate_col], axis=1)
    grad_normed_col = present * inverse_count * grad_mean + dot(grad_projected, column_w, NT)
    grad_middle_col = top + layer_norm_back(grad_normed_col, gain_col, hat_col, inverse_col)
    bsend[:, 0, :] = grad_middle_col
    to_seq(lambda j: bsend.at[j], brecv, 3)
    keep(bsend, brecv, me)

    pack_lane = iota((C, 2 * W), 1)
    pack_row = iota((C, 2 * W), 0)
    grad_full = dot(hat_col, grad_projected, TN)
    mean_hat = fold(jnp.sum(present * hat_col, axis=0, keepdims=True)) * inverse_count
    mean_column = jnp.sum(identity * mean_hat[:, :C], axis=1, keepdims=True)
    grad_col_parts = jnp.concatenate(
        [
            mean_column * grad_query_col[:, :C],
            diagonal_sum(grad_full[:, 0:W]),
            diagonal_sum(grad_full[:, W : 2 * W]),
            diagonal_sum(grad_full[:, 2 * W :]),
            diagonal_sum(dot(gate_col * mixture_col, top, TN)),
        ],
        axis=1,
    )
    placing = jnp.concatenate(
        [
            ones_where(pack_lane == pack_row),
            ones_where(pack_lane == C + pack_row % DH),
            ones_where(pack_lane == C + DH + pack_row % DH),
            ones_where(pack_lane == C + 2 * DH + pack_row),
            ones_where(pack_lane == 2 * C + 2 * DH + pack_row),
        ],
        axis=0,
    )
    pack = pick(grad_col_parts, placing)
    pc_s[...] = pack.reshape(ns, C // ns, 2 * W)
    to_seq(lambda j: pc_s.at[j], pc_r, 4)
    keep(pc_s, pc_r, me)

    wait_all(brecv, 3, ns)
    grad_middle = brecv[:, 0, :]
    grad_gated = dot(grad_middle, out_w, NT)
    grad_gate = grad_gated * mixture * gate_row * (1.0 - gate_row)
    grads_apart = heads_apart(grad_gated * gate_row)
    grad_out_w = dot3(gated, grad_middle, TN)
    grad_rowo = dot(chosen[0], grad_out_w[:, :C]) + dot(chosen[1], grad_out_w[:, C:])

    def bias_core(p):
        return pltpu.make_async_remote_copy(
            src_ref=bias_s.at[p, :, :, 1 - core],
            dst_ref=core_r.at[p],
            send_sem=bias_send.at[0, p],
            recv_sem=bias_recv.at[0, p],
            device_id=(me + 1 - 2 * core, mz),
            device_id_type=MESH,
        )

    def bias_to_x(p):
        bias_core(p).wait()
        x_s[p] = jnp.swapaxes(bias_s[p, :, :, core] + core_r[p], 0, 1)

        def one(i, carry):
            j = lax.rem(mx + i, nx)
            pltpu.make_async_remote_copy(
                src_ref=x_s.at[p, j],
                dst_ref=x_r.at[p, mx],
                send_sem=bias_send.at[1, p],
                recv_sem=bias_recv.at[1, p],
                device_id=((my * nx + j) * 2 + core, mz),
                device_id_type=MESH,
            ).start()
            return carry

        lax.fori_loop(1, nx, one, 0)
        x_r[p, pl.ds(mx, 1)] = x_s[p, pl.ds(mx, 1)]

    def bias_to_y(p):
        part = x_r.at[p, pl.ds(0, nx - 1)]
        wait(part, bias_recv.at[1, p])
        wait(part, bias_send.at[1, p])
        y_s[p] = sum([x_r[p, i] for i in range(1, nx)], x_r[p, 0])

        def one(i, carry):
            j = lax.rem(my + i, ny)
            pltpu.make_async_remote_copy(
                src_ref=y_s.at[p, j],
                dst_ref=y_r.at[p, my],
                send_sem=bias_send.at[2, p],
                recv_sem=bias_recv.at[2, p],
                device_id=((j * nx + mx) * 2 + core, mz),
                device_id_type=MESH,
            ).start()
            return carry

        lax.fori_loop(1, ny, one, 0)
        y_r[p, pl.ds(my, 1)] = y_s[p, pl.ds(my, 1)]

    def bias_done(p):
        part = y_r.at[p, pl.ds(0, ny - 1)]
        wait(part, bias_recv.at[2, p])
        wait(part, bias_send.at[2, p])
        total = sum([y_r[p, i] for i in range(1, ny)], y_r[p, 0])
        gbias_ref[2 * p] = total[:, :res]
        gbias_ref[2 * p + 1] = total[:, res:]

    grad_keys = jnp.zeros((keys, W), F32)
    grad_values = jnp.zeros((keys, W), F32)
    grad_queries = []
    for p in range(PAIRS):
        gh, gl = split2(grads_apart[p])
        grad_weights = dot1(v12, jnp.concatenate([gh, gh], axis=0)) + dot1(v1, gl)
        weights = exps[p] * totals[p]
        inner = jnp.sum(weights * grad_weights, axis=0, keepdims=True)
        grad_scores = weights * (grad_weights - inner)
        bias_s[p] = (grad_scores[:, :half] + grad_scores[:, half:]).reshape(
            ny, nx, 2, block, half
        )
        bias_core(p).start()
        sh, sl = split2(grad_scores)
        wh, wl = split2(weights)
        grad_keys = grad_keys + outer3((sh, sl), query_terms[p][:2])
        grad_values = grad_values + outer3((wh, wl), (gh, gl))
        kh = key_high[32 * p : 32 * p + 32]
        kl = key_low[32 * p : 32 * p + 32]
        grad_queries.append(
            heads_together(dot1(kh, sh) + (dot1(kl, sh) + dot1(kh, sl)))
        )

    grad_memory = jnp.concatenate([grad_keys, grad_values], axis=1)
    grad_query = jnp.concatenate(grad_queries, axis=0).T * scaling
    own_grads = jnp.concatenate([grad_query, grad_gate], axis=1)
    gh, gl = split2(grad_memory)
    grad_memory_w = dot1(hat_high, gh) + (dot1(hat_high, gl) + dot1(hat_low, gh))
    grad_own_w = dot3(hat_local, own_grads, TN)
    grad_parts = (
        grad_own_w[:, :W],
        grad_memory_w[:, :W],
        grad_memory_w[:, W:],
        grad_own_w[:, W:],
    )
    gathered = pick(
        jnp.concatenate([part[:C] for part in grad_parts], axis=0), chosen[0], NT
    ) + pick(jnp.concatenate([part[C:] for part in grad_parts], axis=0), chosen[1], NT)
    pack_row_part = jnp.concatenate(
        [gathered[i * C : (i + 1) * C] for i in range(4)] + [grad_rowo, jnp.zeros((C, C), F32)],
        axis=1,
    )
    pr_s[...] = pack_row_part.reshape(ns, C // ns, 3 * W)
    to_seq(lambda j: pr_s.at[j], pr_r, 6)
    keep(pr_s, pr_r, me)

    for p in range(PAIRS):
        bias_to_x(p)
    wait_all(pc_r, 4, ns)
    tc_s[...] = jnp.sum(pc_r[...], axis=0)
    to_res(lambda j: tc_s, tc_r, 9)
    tc_r[pl.ds(mz, 1)] = tc_s[...][None]
    own_normed_grad = dot(own_grads, jnp.concatenate([query_w, gate_w], axis=1), NT)
    zr_s[...] = dot3(grad_memory, memory_w, NT).reshape(nz, res, W)
    keep(zr_s, zr_r, mz)
    wait_all(tc_r, 9, nz)
    oc_r[me] = sum([tc_r[i] for i in range(1, nz)], tc_r[0])
    to_seq(lambda j: oc_r.at[me], oc_r, 10)

    wait_all(pr_r, 6, ns)
    t_s[...] = jnp.sum(pr_r[...], axis=0)
    to_res(lambda j: t_s, t_r, 7)
    t_r[pl.ds(mz, 1)] = t_s[...][None]
    to_res(lambda j: zr_s.at[j], zr_r, 5)
    for p in range(PAIRS):
        bias_to_y(p)

    wait_all(t_r, 7, nz)
    o_r[me] = sum([t_r[i] for i in range(1, nz)], t_r[0])
    to_seq(lambda j: o_r.at[me], o_r, 8)

    wait_all(zr_r, 5, nz)
    grad_normed_row = sum([zr_r[i] for i in range(1, nz)], zr_r[0]) + own_normed_grad
    grad_initial = layer_norm_back(grad_normed_row, gain_row, hat_local, inverse_local)
    grad_align = (grad_middle + grad_initial).astype(BF16)
    galign_ref[0] = grad_align[:, :C]
    galign_ref[1] = grad_align[:, C:]
    stores[0].start()
    for p in range(PAIRS):
        bias_done(p)
    stores[1].start()
    gather_finish()
    gain_columns = [
        jnp.sum(identity * gains[i : i + 1], axis=1, keepdims=True) for i in range(2)
    ]

    def gain_gradient(part, weights):
        column_sum = jnp.sum(part * weights, axis=1, keepdims=True)
        return jnp.sum(identity * column_sum, axis=0, keepdims=True)

    wait_all(oc_r, 10, ns)
    final = oc_r[...].reshape(C, 2 * W)
    part = final[:, 0 : 2 * C + 2 * DH]
    gcolp_ref[...] = part * gain_columns[1]
    gcolo_ref[...] = final[:, 2 * C + 2 * DH : 3 * C + 2 * DH]
    ggains_ref[1:2, :] = gain_gradient(part, colp)
    stores[5].start()
    stores[6].start()

    wait_all(o_r, 8, ns)
    final = o_r[...].reshape(C, 3 * W)
    part = final[:, 0 : 4 * C]
    growp_ref[...] = part * gain_columns[0]
    growo_ref[...] = final[:, 4 * C : 5 * C]
    stores[3].start()
    stores[4].start()
    ggains_ref[0:1, :] = gain_gradient(part, rowp)
    stores[2].start()
    for store in stores:
        store.wait()


def store_all(*refs):
    count = (len(refs) - 1) // 2
    semaphores = refs[-1]
    copies = [
        pltpu.make_async_copy(refs[i], refs[count + i], semaphores.at[i]) for i in range(count)
    ]
    for copy in copies:
        copy.start()
    for copy in copies:
        copy.wait()


def finish(arrays):
    arrays = pl.pallas_call(
        store_all,
        out_shape=tuple(jax.ShapeDtypeStruct(a.shape, a.dtype) for a in arrays),
        in_specs=[pl.BlockSpec(memory_space=pltpu.VMEM)] * len(arrays),
        out_specs=(pl.BlockSpec(memory_space=pltpu.HBM),) * len(arrays),
        scratch_shapes=[pltpu.SemaphoreType.DMA((len(arrays),))],
    )(*arrays)
    return (arrays[0], jnp.swapaxes(arrays[1], 1, 2)) + tuple(arrays[2:])


def solution(mesh):
    seq_devices = mesh.shape["seq"]
    res_devices = mesh.shape["res"]
    nx = 4 if seq_devices == 64 else 2
    ny = seq_devices // (2 * nx)
    nz = res_devices
    res = seq_devices
    keys = nz * res
    block = keys // seq_devices
    half = 2 * res

    def local(
        alignment,
        cotangent,
        pair_bias,
        norm_gains,
        row_project,
        row_output,
        column_project,
        column_output,
        residue_mask,
        sequence_mask,
    ):
        ns = seq_devices
        chunk = C // ns
        outs = pl.pallas_call(
            functools.partial(kernel, (ny, nx, nz)),
            out_shape=(
                jax.ShapeDtypeStruct((L, res, C), BF16),
                jax.ShapeDtypeStruct((H, block, res), F32),
                jax.ShapeDtypeStruct((2, C), F32),
                jax.ShapeDtypeStruct((C, 4 * C), F32),
                jax.ShapeDtypeStruct((C, C), F32),
                jax.ShapeDtypeStruct((C, 2 * C + 2 * DH), F32),
                jax.ShapeDtypeStruct((C, C), F32),
            ),
            in_specs=[pl.BlockSpec(memory_space=pltpu.HBM)] * 10,
            out_specs=(pl.BlockSpec(memory_space=pltpu.HBM),) * 7,
            scratch_shapes=[
                pltpu.VMEM((nz, res + 8, W), F32),
                pltpu.VMEM((ns, 1, 2 * W), F32),
                pltpu.VMEM((ns, 1, 2 * W), F32),
                pltpu.VMEM((ns, 1, W), F32),
                pltpu.VMEM((ns, 1, W), F32),
                pltpu.VMEM((ns, 1, W), F32),
                pltpu.VMEM((ns, 1, W), F32),
                pltpu.VMEM((PAIRS, keys, half), F32),
                pltpu.VMEM((PAIRS, keys, 2 * half), F32),
                pltpu.VMEM((PAIRS, ny, nx, 2, block, half), F32),
                pltpu.VMEM((PAIRS, ny, nx, block, half), F32),
                pltpu.VMEM((PAIRS, nx, ny, block, half), F32),
                pltpu.VMEM((PAIRS, nx, ny, block, half), F32),
                pltpu.VMEM((PAIRS, ny, block, half), F32),
                pltpu.VMEM((PAIRS, ny, block, half), F32),
                pltpu.VMEM((nz, res, W), F32),
                pltpu.VMEM((nz, res, W), F32),
                pltpu.VMEM((ns, chunk, 2 * W), F32),
                pltpu.VMEM((ns, chunk, 2 * W), F32),
                pltpu.VMEM((ns, chunk, 3 * W), F32),
                pltpu.VMEM((ns, chunk, 3 * W), F32),
                pltpu.VMEM((chunk, 3 * W), F32),
                pltpu.VMEM((nz, chunk, 3 * W), F32),
                pltpu.VMEM((ns, chunk, 3 * W), F32),
                pltpu.VMEM((chunk, 2 * W), F32),
                pltpu.VMEM((nz, chunk, 2 * W), F32),
                pltpu.VMEM((ns, chunk, 2 * W), F32),
                pltpu.VMEM((L, res, C), BF16),
                pltpu.VMEM((L, res, C), BF16),
                pltpu.VMEM((H, res, keys), BF16),
                pltpu.VMEM((2, C), F32),
                pltpu.VMEM((C, 4 * C), F32),
                pltpu.VMEM((C, C), F32),
                pltpu.VMEM((C, 2 * C + 2 * DH), F32),
                pltpu.VMEM((C, C), F32),
                pltpu.VMEM((1, res), jnp.int32),
                pltpu.VMEM((1, L), jnp.int32),
                pltpu.SemaphoreType.DMA((11,)),
                pltpu.SemaphoreType.DMA((11,)),
                pltpu.SemaphoreType.DMA((3, PAIRS)),
                pltpu.SemaphoreType.DMA((3, PAIRS)),
                pltpu.SemaphoreType.DMA((10,)),
                pltpu.SemaphoreType.DMA((8,)),
                pltpu.SemaphoreType.DMA((8,)),
                pltpu.VMEM((L, res, C), BF16),
                pltpu.VMEM((H, block, res), F32),
                pltpu.VMEM((2, C), F32),
                pltpu.VMEM((C, 4 * C), F32),
                pltpu.VMEM((C, C), F32),
                pltpu.VMEM((C, 2 * C + 2 * DH), F32),
                pltpu.VMEM((C, C), F32),
                pltpu.SemaphoreType.DMA((7,)),
            ],
            compiler_params=pltpu.CompilerParams(
                collective_id=0, has_side_effects=True, vmem_limit_bytes=64 * 1024 * 1024
            ),
        )(
            alignment,
            cotangent,
            pair_bias,
            norm_gains,
            row_project,
            row_output,
            column_project,
            column_output,
            residue_mask[None],
            sequence_mask[None],
        )
        return finish(outs)

    placed = (
        P("seq", "res", None),
        P("seq", "res", None),
        P(None, "res", None),
        P(),
        P(),
        P(),
        P(),
        P(),
        P("res"),
        P("seq"),
    )
    return jax.shard_map(
        local,
        mesh=mesh,
        in_specs=placed,
        out_specs=(P("seq", "res", None), P(None, "res", "seq"), P(), P(), P(), P(), P()),
        check_vma=False,
    )
```

```python
import functools
import jax
import jax.numpy as jnp
from jax import lax
from jax.experimental import pallas as pl
from jax.experimental.pallas import tpu as pltpu
from jax.sharding import PartitionSpec as P

C = 64
H = 8
DH = 8
L = 2
PAIRS = 4
W = 128
EPSILON = 1e-05
MASKED = 1000000000.0
F32 = jnp.float32
BF16 = jnp.bfloat16
MESH = pl.DeviceIdType.MESH
NN = (((1,), (0,)), ((), ()))
NT = (((1,), (1,)), ((), ()))
TN = (((0,), (0,)), ((), ()))


def dot(a, b, dims=NN):
    return lax.dot_general(
        a, b, dims, precision=lax.Precision.HIGHEST, preferred_element_type=F32
    )


def dot1(a, b, dims=NN):
    return lax.dot_general(a, b, dims, preferred_element_type=F32)


def split2(a):
    high = a.astype(BF16)
    return high, (a - high.astype(F32)).astype(BF16)


def split3(a):
    high = a.astype(BF16)
    rest = a - high.astype(F32)
    middle = rest.astype(BF16)
    return high, middle, (rest - middle.astype(F32)).astype(BF16)


def dot3(a, b, dims=NN):
    ah, al = split2(a)
    bh, bl = split2(b)
    return dot1(ah, bh, dims) + (dot1(ah, bl, dims) + dot1(al, bh, dims))


def products(first, second):
    a1, a2, a3 = first
    b1, b2, b3 = second
    a12 = jnp.concatenate([a1, a2], axis=1)
    a13 = jnp.concatenate([a1, a3], axis=1)
    return dot1(a12, jnp.concatenate([b1, b1], axis=0)) + (
        dot1(a12, jnp.concatenate([b2, b2], axis=0)) + dot1(a13, jnp.concatenate([b3, b1], axis=0))
    )


def pick(values, ones, dims=NN):
    ones = ones.astype(BF16)
    axis = dims[0][1][0]
    return dot1(
        jnp.concatenate(split2(values), axis=1), jnp.concatenate([ones, ones], axis=axis), dims
    )


def outer3(left, right):
    lh, ll = left
    rh, rl = right
    both = dot1(lh, jnp.concatenate([rh, rl], axis=0), NT)
    count = rh.shape[0]
    return both[:, :count] + (both[:, count:] + dot1(ll, rh, NT))


def iota(shape, axis):
    return lax.broadcasted_iota(jnp.int32, shape, axis)


def ones_where(condition):
    return jnp.where(condition, 1.0, 0.0).astype(F32)


def twice(row):
    return jnp.concatenate([row, row], axis=1)


def fold(row):
    return row + jnp.concatenate([row[:, C:], row[:, :C]], axis=1)


def block_diagonal(weights):
    zero = jnp.zeros_like(weights)
    return jnp.concatenate(
        [jnp.concatenate([weights, zero], axis=1), jnp.concatenate([zero, weights], axis=1)], axis=0
    )


def diagonal_sum(full):
    return full[:C, :C] + full[C:, C:]


def kernel(
    sizes,
    align_hbm,
    cot_hbm,
    bias_hbm,
    gains_hbm,
    rowp_hbm,
    rowo_hbm,
    colp_hbm,
    colo_hbm,
    rmask_hbm,
    smask_hbm,
    galign_hbm,
    gbias_hbm,
    ggains_hbm,
    growp_hbm,
    growo_hbm,
    gcolp_hbm,
    gcolo_hbm,
    xall,
    gsend,
    grecv,
    msend,
    mrecv,
    bsend,
    brecv,
    bias_t,
    exps,
    exps_high,
    exps_low,
    bias_s,
    core_r,
    x_s,
    x_r,
    y_s,
    y_r,
    zr_s,
    zr_r,
    pc_s,
    pc_r,
    pr_s,
    pr_r,
    t_s,
    t_r,
    o_r,
    tc_s,
    tc_r,
    oc_r,
    align_ref,
    cot_ref,
    bias_ref,
    gains_ref,
    rowp_ref,
    rowo_ref,
    colp_ref,
    colo_ref,
    rmask_ref,
    smask_ref,
    send_sem,
    recv_sem,
    bias_send,
    bias_recv,
    load_sem,
    gather_send,
    gather_recv,
    galign_ref,
    gbias_ref,
    ggains_ref,
    growp_ref,
    growo_ref,
    gcolp_ref,
    gcolo_ref,
    store_sem,
):
    ny, nx, nz = sizes
    ns = ny * nx * 2
    res = ns
    keys = nz * res
    wide = 4 * res
    half = 2 * res
    block = keys // ns
    me = lax.axis_index("seq")
    mz = lax.axis_index("res")
    core = lax.rem(me, 2)
    mx = lax.rem(me // 2, nx)
    my = me // (2 * nx)
    scaling = DH ** (-0.5)

    sources = (
        align_hbm,
        rmask_hbm,
        smask_hbm,
        cot_hbm,
        gains_hbm,
        rowp_hbm,
        rowo_hbm,
        bias_hbm,
        colp_hbm,
        colo_hbm,
    )
    targets = (
        align_ref,
        rmask_ref,
        smask_ref,
        cot_ref,
        gains_ref,
        rowp_ref,
        rowo_ref,
        bias_ref,
        colp_ref,
        colo_ref,
    )
    loads = [
        pltpu.make_async_copy(source, target, load_sem.at[i])
        for i, (source, target) in enumerate(zip(sources, targets))
    ]
    for load in loads:
        load.start()

    barrier = pltpu.get_barrier_semaphore()

    def greet_seq(i, carry):
        pl.semaphore_signal(
            barrier, inc=1, device_id=(lax.rem(me + i, ns), mz), device_id_type=MESH
        )
        return carry

    def greet_res(i, carry):
        pl.semaphore_signal(
            barrier, inc=1, device_id=(me, lax.rem(mz + i, nz)), device_id_type=MESH
        )
        return carry

    lax.fori_loop(1, nz, greet_res, 0)
    lax.fori_loop(ns // 4, ns, greet_seq, 0)
    lax.fori_loop(1, ns // 4, greet_seq, 0)

    stores = [
        pltpu.make_async_copy(source, target, store_sem.at[i])
        for i, (source, target) in enumerate(
            (
                (galign_ref, galign_hbm),
                (gbias_ref, gbias_hbm),
                (ggains_ref, ggains_hbm),
                (growp_ref, growp_hbm),
                (growo_ref, growo_hbm),
                (gcolp_ref, gcolp_hbm),
                (gcolo_ref, gcolo_hbm),
            )
        )
    ]

    def to_seq(source, target, which):
        def one(i, carry):
            j = lax.rem(me + i, ns)
            pltpu.make_async_remote_copy(
                src_ref=source(j),
                dst_ref=target.at[me],
                send_sem=send_sem.at[which],
                recv_sem=recv_sem.at[which],
                device_id=(j, mz),
                device_id_type=MESH,
            ).start()
            return carry

        lax.fori_loop(ns // 4, ns, one, 0)
        lax.fori_loop(1, ns // 4, one, 0)

    def to_res(source, target, which):
        def one(i, carry):
            j = lax.rem(mz + i, nz)
            pltpu.make_async_remote_copy(
                src_ref=source(j),
                dst_ref=target.at[mz],
                send_sem=send_sem.at[which],
                recv_sem=recv_sem.at[which],
                device_id=(me, j),
                device_id_type=MESH,
            ).start()
            return carry

        lax.fori_loop(1, nz, one, 0)

    def wait(ref, semaphore):
        pltpu.make_async_copy(ref, ref, semaphore).wait()

    def wait_all(buffer, which, count):
        part = buffer.at[pl.ds(0, count - 1)]
        wait(part, recv_sem.at[which])
        wait(part, send_sem.at[which])

    def keep(source, target, at):
        target[pl.ds(at, 1)] = source[pl.ds(at, 1)]

    ring = (3, nz - 3, 2, nz - 2, 1, nz - 1)
    cut = (res + 8) // 16 * 8

    def gather_copy(step):
        return pltpu.make_async_remote_copy(
            src_ref=xall.at[mz],
            dst_ref=xall.at[mz],
            send_sem=gather_send.at[step],
            recv_sem=gather_recv.at[step],
            device_id=(me, lax.rem(mz + step, nz)),
            device_id_type=MESH,
        )

    def gather_relay(step, rows, semaphore):
        part = xall.at[lax.rem(mz + nz - step, nz), rows]
        return pltpu.make_async_remote_copy(
            src_ref=part,
            dst_ref=part,
            send_sem=gather_send.at[semaphore],
            recv_sem=gather_recv.at[semaphore],
            device_id=(me, lax.rem(mz + (nz // 2 - step) + nz, nz)),
            device_id_type=MESH,
        )

    relays = ((3, pl.ds(0, cut), 0), (nz - 3, pl.ds(cut, res + 8 - cut), 4))

    def gather_start():
        if nz != 8:
            to_res(lambda j: xall.at[mz], xall, 0)
            return
        for step in ring:
            gather_copy(step).start()

    def gather_pass_on():
        if nz != 8:
            return
        for step, rows, semaphore in relays:
            gather_copy(step).wait_recv()
            gather_relay(step, rows, semaphore).start()

    def gather_wait():
        if nz != 8:
            wait_all(xall, 0, nz)
            return
        for step in ring[2:]:
            gather_copy(step).wait_recv()
        for relay in relays:
            gather_relay(*relay).wait_recv()

    def gather_finish():
        if nz != 8:
            return
        for step in ring:
            gather_copy(step).wait_send()
        for relay in relays:
            gather_relay(*relay).wait_send()

    for load in loads[:4]:
        load.wait()
    align = align_ref[...].astype(F32)
    initial = jnp.concatenate([align[0], align[1]], axis=1)
    cot = cot_ref[...].astype(F32)
    top_local = jnp.concatenate([cot[0], cot[1]], axis=1)
    averaging = ones_where(iota((W, W), 0) // C == iota((W, W), 1) // C) * (1.0 / C)

    def layer_norm(values):
        centred = values - dot(values, averaging)
        spread = dot(centred * centred, averaging)
        inverse = lax.rsqrt(spread + EPSILON)
        return centred * inverse, inverse

    def layer_norm_back(grad_normed, gain, hat, inverse):
        scaled = grad_normed * gain
        rows = scaled.shape[0]
        means = dot(jnp.concatenate([scaled, scaled * hat], axis=0), averaging)
        return inverse * (scaled - means[:rows] - hat * means[rows:])

    hat_local, inverse_local = layer_norm(initial)
    xall[mz, 0:res, :] = hat_local
    xall[mz, res : res + 8, :] = jnp.broadcast_to(
        jnp.concatenate([rmask_ref[...].astype(F32), jnp.zeros((1, W - res), F32)], axis=1), (8, W)
    )
    present_pair = smask_ref[...].astype(F32)
    present_row = jnp.concatenate(
        [jnp.broadcast_to(present_pair[:, i : i + 1], (1, C)) for i in range(L)], axis=1
    )
    gsend[:, 0, 0:W] = top_local
    gsend[:, 0, W : 2 * W] = jnp.broadcast_to(present_row, (res, W))

    pl.semaphore_wait(barrier, ns + nz - 2)
    gather_start()
    to_seq(lambda j: gsend.at[j], grecv, 1)
    keep(gsend, grecv, me)

    for load in loads[4:]:
        load.wait()
    gains = gains_ref[...]
    gain_row = twice(gains[0:1])
    gain_col = twice(gains[1:2])

    lane = iota((C, W), 1)
    column = (lane // 32) * 16 + lane % 16
    chosen = [
        ones_where((iota((C, W), 0) == column) & ((lane // 16) % 2 == s)) for s in range(L)
    ]

    def spread_columns(weights):
        return jnp.concatenate([dot(weights, chosen[0]), dot(weights, chosen[1])], axis=0)

    rowp = rowp_ref[...]
    query_w = spread_columns(rowp[:, 0:C])
    key_w = spread_columns(rowp[:, C : 2 * C])
    value_w = spread_columns(rowp[:, 2 * C : 3 * C])
    gate_w = spread_columns(rowp[:, 3 * C :])
    rowo = rowo_ref[...]
    out_w = jnp.concatenate([dot(chosen[0], rowo, TN), dot(chosen[1], rowo, TN)], axis=1)
    memory_w = jnp.concatenate([key_w, value_w], axis=1)

    normed_local = hat_local * gain_row
    queries = dot(normed_local, query_w) * scaling
    gate_row = jax.nn.sigmoid(dot(normed_local, gate_w))

    gather_pass_on()
    for p in range(PAIRS):
        pair = bias_ref[2 * p : 2 * p + 2].astype(F32).reshape(half, keys)
        bias_t[p] = pair.T

    mine = ones_where(iota((32, wide), 0) // DH == iota((32, wide), 1) // res)
    nothing = jnp.zeros((32, wide), BF16)
    group = iota((keys, W), 1) // 32

    def heads_apart(rows):
        flat = rows.T
        flat = jnp.concatenate([flat, flat, flat, flat], axis=1)
        return [flat[32 * p : 32 * p + 32] * mine for p in range(PAIRS)]

    def placed(part, p):
        return jnp.concatenate([part if i == p else nothing for i in range(PAIRS)], axis=0)

    def turns(part):
        part = part.astype(F32)
        return [part] + [pltpu.roll(part, 32 * i, 1) for i in range(1, PAIRS)]

    def lanes_of(p, *parts):
        found = parts[-1][(len(parts) - 1 - p) % PAIRS]
        for i in reversed(range(len(parts) - 1)):
            found = jnp.where(group == i, parts[i][(i - p) % PAIRS], found)
        return found.astype(BF16)

    query_parts = [split3(apart) for apart in heads_apart(queries)]
    query_stacks = [
        jnp.concatenate([q1, q2, q1, q2, q3, q1, nothing, nothing], axis=0)
        for q1, q2, q3 in query_parts
    ]

    def heads_together(apart):
        kept = apart * mine
        both = kept[:, :half] + kept[:, half:]
        return both[:, :res] + both[:, res:]

    identity = ones_where(iota((C, C), 0) == iota((C, C), 1))
    colp = colp_ref[...]
    colo = colo_ref[...]
    entry = iota((C + 2 * DH + C, C), 0)
    entry_lane = iota((C + 2 * DH + C, C), 1)
    key_col_w = block_diagonal(dot(colp, ones_where(entry == C + entry_lane % DH)))
    value_col_w = block_diagonal(dot(colp, ones_where(entry == C + DH + entry_lane % DH)))
    gate_col_w = block_diagonal(dot(colp, ones_where(entry == C + 2 * DH + entry_lane)))
    query_col_w = block_diagonal(colp[:, 0:C])
    out_col_w = block_diagonal(colo)
    column_w = jnp.concatenate([key_col_w, value_col_w, gate_col_w], axis=1)
    head_sum = ones_where(iota((W, W), 0) // DH == iota((W, W), 1) // DH)

    gather_wait()
    hat_all = xall[:, 0:res, :].reshape(keys, W)
    normed_all = hat_all * gain_row
    memory = products(split3(normed_all), split3(memory_w))
    key_rows = memory[:, :W]
    value_rows = memory[:, W:]
    value_flat = value_rows.T
    mask_flat = jnp.concatenate([xall[z, res : res + 8, :] for z in range(nz)], axis=0).T
    key_bias = jnp.concatenate(
        [MASKED * (mask_flat[:res, 8 * z : 8 * z + 1] - 1.0) for z in range(nz)], axis=0
    )
    t1, t2, t3 = [turns(part) for part in split3(key_rows)]
    value_high, value_low = split2(value_flat)

    totals = []
    mixed = []
    for p in range(PAIRS):
        key_stack = jnp.concatenate([lanes_of(p, t1, t1, t2, t2), lanes_of(p, t1, t3)], axis=1)
        scores = dot1(key_stack, query_stacks[p])
        scores = scores + twice(bias_t[p]) + key_bias
        peak = jnp.max(scores, axis=0, keepdims=True)
        exponent = jnp.exp(scores - peak)
        exps[p] = exponent
        inverse_total = 1.0 / jnp.sum(exponent, axis=0, keepdims=True)
        totals.append(inverse_total)
        eh, el = split2(exponent)
        exps_high[p] = eh
        exps_low[p] = el
        vh = value_high[32 * p : 32 * p + 32]
        vl = value_low[32 * p : 32 * p + 32]
        apart = dot1(vh, eh) + (dot1(vl, eh) + dot1(vh, el))
        mixed.append(heads_together(apart * inverse_total))
    mixture = jnp.concatenate(mixed, axis=0).T
    gated = gate_row * mixture
    middle = initial + dot(gated, out_w)
    msend[:, 0, :] = middle
    to_seq(lambda j: msend.at[j], mrecv, 2)
    keep(msend, mrecv, me)

    key_flat = key_rows.T
    key_high, key_low = split2(key_flat)

    wait_all(grecv, 1, ns)
    top = grecv[:, 0, 0:W]
    present = grecv[:, 0, W : 2 * W]
    counted = jnp.sum(fold(jnp.sum(present, axis=0, keepdims=True)), axis=1, keepdims=True) * (
        1.0 / W
    )
    inverse_count = 1.0 / counted
    grad_gated_col = dot(top, out_col_w, NT)

    wait_all(mrecv, 2, ns)
    hat_col, inverse_col = layer_norm(mrecv[:, 0, :])
    normed_col = hat_col * gain_col
    mean_normed = fold(jnp.sum(present * normed_col, axis=0, keepdims=True)) * inverse_count
    queries_col = dot(mean_normed, query_col_w) * scaling
    projected = dot(normed_col, column_w)
    key_col = projected[:, 0:W]
    value_col = projected[:, W : 2 * W]
    gate_col = jax.nn.sigmoid(projected[:, 2 * W :])
    scores_col = dot(key_col * queries_col, head_sum) + MASKED * (present - 1.0)
    peak_row = jnp.max(scores_col, axis=0, keepdims=True)
    peak_row = jnp.maximum(peak_row, jnp.concatenate([peak_row[:, C:], peak_row[:, :C]], axis=1))
    exp_col = jnp.exp(scores_col - peak_row)
    weights_col = exp_col * (1.0 / fold(jnp.sum(exp_col, axis=0, keepdims=True)))
    mixture_col = fold(jnp.sum(weights_col * value_col, axis=0, keepdims=True))
    grad_mixture_col = fold(jnp.sum(gate_col * grad_gated_col, axis=0, keepdims=True))
    grad_gate_col = grad_gated_col * mixture_col * gate_col * (1.0 - gate_col)
    grad_weights_col = dot(value_col * grad_mixture_col, head_sum)
    inner_col = fold(jnp.sum(weights_col * grad_weights_col, axis=0, keepdims=True))
    grad_scores_col = weights_col * (grad_weights_col - inner_col)
    grad_query_col = fold(jnp.sum(grad_scores_col * key_col, axis=0, keepdims=True)) * scaling
    grad_key_col = grad_scores_col * queries_col
    grad_value_col = weights_col * grad_mixture_col
    grad_mean = dot(grad_query_col, query_col_w, NT)
    grad_projected = jnp.concatenate([grad_key_col, grad_value_col, grad_gate_col], axis=1)
    grad_normed_col = present * inverse_count * grad_mean + dot(grad_projected, column_w, NT)
    grad_middle_col = top + layer_norm_back(grad_normed_col, gain_col, hat_col, inverse_col)
    bsend[:, 0, :] = grad_middle_col
    to_seq(lambda j: bsend.at[j], brecv, 3)
    keep(bsend, brecv, me)

    pack_lane = iota((C, 2 * W), 1)
    pack_row = iota((C, 2 * W), 0)
    grad_full = dot(hat_col, grad_projected, TN)
    mean_hat = fold(jnp.sum(present * hat_col, axis=0, keepdims=True)) * inverse_count
    mean_column = jnp.sum(identity * mean_hat[:, :C], axis=1, keepdims=True)
    grad_col_parts = jnp.concatenate(
        [
            mean_column * grad_query_col[:, :C],
            diagonal_sum(grad_full[:, 0:W]),
            diagonal_sum(grad_full[:, W : 2 * W]),
            diagonal_sum(grad_full[:, 2 * W :]),
            diagonal_sum(dot(gate_col * mixture_col, top, TN)),
        ],
        axis=1,
    )
    placing = jnp.concatenate(
        [
            ones_where(pack_lane == pack_row),
            ones_where(pack_lane == C + pack_row % DH),
            ones_where(pack_lane == C + DH + pack_row % DH),
            ones_where(pack_lane == C + 2 * DH + pack_row),
            ones_where(pack_lane == 2 * C + 2 * DH + pack_row),
        ],
        axis=0,
    )
    pack = pick(grad_col_parts, placing)
    pc_s[...] = pack.reshape(ns, C // ns, 2 * W)
    to_seq(lambda j: pc_s.at[j], pc_r, 4)
    keep(pc_s, pc_r, me)

    v1, v2 = [turns(part) for part in split2(value_rows)]
    hat_high, hat_low = split2(hat_all.T)
    value_stacks = [lanes_of(p, v1, v2, v1) for p in range(PAIRS)]

    wait_all(brecv, 3, ns)
    grad_middle = brecv[:, 0, :]
    grad_gated = dot(grad_middle, out_w, NT)
    grad_gate = grad_gated * mixture * gate_row * (1.0 - gate_row)
    grads_apart = heads_apart(grad_gated * gate_row)
    grad_out_w = dot3(gated, grad_middle, TN)
    grad_rowo = dot(chosen[0], grad_out_w[:, :C]) + dot(chosen[1], grad_out_w[:, C:])

    def bias_core(p):
        return pltpu.make_async_remote_copy(
            src_ref=bias_s.at[p, :, :, 1 - core],
            dst_ref=core_r.at[p],
            send_sem=bias_send.at[0, p],
            recv_sem=bias_recv.at[0, p],
            device_id=(me + 1 - 2 * core, mz),
            device_id_type=MESH,
        )

    def bias_to_x(p):
        bias_core(p).wait()
        x_s[p] = jnp.swapaxes(bias_s[p, :, :, core] + core_r[p], 0, 1)

        def one(i, carry):
            j = lax.rem(mx + i, nx)
            pltpu.make_async_remote_copy(
                src_ref=x_s.at[p, j],
                dst_ref=x_r.at[p, mx],
                send_sem=bias_send.at[1, p],
                recv_sem=bias_recv.at[1, p],
                device_id=((my * nx + j) * 2 + core, mz),
                device_id_type=MESH,
            ).start()
            return carry

        lax.fori_loop(1, nx, one, 0)
        x_r[p, pl.ds(mx, 1)] = x_s[p, pl.ds(mx, 1)]

    def bias_to_y(p):
        part = x_r.at[p, pl.ds(0, nx - 1)]
        wait(part, bias_recv.at[1, p])
        wait(part, bias_send.at[1, p])
        y_s[p] = sum([x_r[p, i] for i in range(1, nx)], x_r[p, 0])

        def one(i, carry):
            j = lax.rem(my + i, ny)
            pltpu.make_async_remote_copy(
                src_ref=y_s.at[p, j],
                dst_ref=y_r.at[p, my],
                send_sem=bias_send.at[2, p],
                recv_sem=bias_recv.at[2, p],
                device_id=((j * nx + mx) * 2 + core, mz),
                device_id_type=MESH,
            ).start()
            return carry

        lax.fori_loop(1, ny, one, 0)
        y_r[p, pl.ds(my, 1)] = y_s[p, pl.ds(my, 1)]

    def bias_done(p):
        part = y_r.at[p, pl.ds(0, ny - 1)]
        wait(part, bias_recv.at[2, p])
        wait(part, bias_send.at[2, p])
        total = sum([y_r[p, i] for i in range(1, ny)], y_r[p, 0])
        gbias_ref[2 * p] = total[:, :res]
        gbias_ref[2 * p + 1] = total[:, res:]

    score_parts = []
    value_parts = []
    grad_queries = []
    for p in range(PAIRS):
        gh, gl = split2(grads_apart[p] * totals[p])
        grad_weights = dot1(value_stacks[p], jnp.concatenate([gh, gh, gl, nothing], axis=0))
        exponent = exps[p]
        inner = jnp.sum(exponent * grad_weights, axis=0, keepdims=True) * totals[p]
        grad_scores = exponent * (grad_weights - inner)
        bias_s[p] = (grad_scores[:, :half] + grad_scores[:, half:]).reshape(
            ny, nx, 2, block, half
        )
        bias_core(p).start()
        sh, sl = split2(grad_scores)
        score_parts.append((sh, sl))
        value_parts.append((gh, gl))
        kh = key_high[32 * p : 32 * p + 32]
        kl = key_low[32 * p : 32 * p + 32]
        grad_queries.append(
            heads_together(dot1(kh, sh) + (dot1(kl, sh) + dot1(kh, sl)))
        )

    empty = jnp.zeros((W, wide), BF16)

    def outer_all(lefts, rights):
        left = jnp.concatenate([part for pair in lefts for part in pair], axis=1)
        highs = [placed(rh, p) for p, (rh, _) in enumerate(rights)]
        lows = [placed(rl, p) for p, (_, rl) in enumerate(rights)]
        right = jnp.concatenate(
            [
                jnp.concatenate([part for high in highs for part in (high, high)], axis=1),
                jnp.concatenate([part for low in lows for part in (low, empty)], axis=1),
            ],
            axis=0,
        )
        both = dot1(left, right, NT)
        return both[:, :W] + both[:, W:]

    grad_keys = outer_all(score_parts, [parts[:2] for parts in query_parts])
    grad_values = outer_all([(exps_high[p], exps_low[p]) for p in range(PAIRS)], value_parts)

    grad_memory = jnp.concatenate([grad_keys, grad_values], axis=1)
    grad_query = jnp.concatenate(grad_queries, axis=0).T * scaling
    own_grads = jnp.concatenate([grad_query, grad_gate], axis=1)
    gh, gl = split2(grad_memory)
    grad_memory_w = dot1(hat_high, gh) + (dot1(hat_high, gl) + dot1(hat_low, gh))
    grad_own_w = dot3(hat_local, own_grads, TN)
    grad_parts = (
        grad_own_w[:, :W],
        grad_memory_w[:, :W],
        grad_memory_w[:, W:],
        grad_own_w[:, W:],
    )
    gathered = pick(
        jnp.concatenate([part[:C] for part in grad_parts], axis=0), chosen[0], NT
    ) + pick(jnp.concatenate([part[C:] for part in grad_parts], axis=0), chosen[1], NT)
    pack_row_part = jnp.concatenate(
        [gathered[i * C : (i + 1) * C] for i in range(4)] + [grad_rowo, jnp.zeros((C, C), F32)],
        axis=1,
    )
    pr_s[...] = pack_row_part.reshape(ns, C // ns, 3 * W)
    to_seq(lambda j: pr_s.at[j], pr_r, 6)
    keep(pr_s, pr_r, me)

    for p in range(PAIRS):
        bias_to_x(p)
    wait_all(pc_r, 4, ns)
    tc_s[...] = jnp.sum(pc_r[...], axis=0)
    to_res(lambda j: tc_s, tc_r, 9)
    tc_r[pl.ds(mz, 1)] = tc_s[...][None]
    own_normed_grad = dot(own_grads, jnp.concatenate([query_w, gate_w], axis=1), NT)
    zr_s[...] = dot3(grad_memory, memory_w, NT).reshape(nz, res, W)
    keep(zr_s, zr_r, mz)
    wait_all(tc_r, 9, nz)
    oc_r[me] = sum([tc_r[i] for i in range(1, nz)], tc_r[0])
    to_seq(lambda j: oc_r.at[me], oc_r, 10)

    wait_all(pr_r, 6, ns)
    t_s[...] = jnp.sum(pr_r[...], axis=0)
    to_res(lambda j: t_s, t_r, 7)
    t_r[pl.ds(mz, 1)] = t_s[...][None]
    to_res(lambda j: zr_s.at[j], zr_r, 5)
    for p in range(PAIRS):
        bias_to_y(p)

    wait_all(t_r, 7, nz)
    o_r[me] = sum([t_r[i] for i in range(1, nz)], t_r[0])
    to_seq(lambda j: o_r.at[me], o_r, 8)

    wait_all(zr_r, 5, nz)
    grad_normed_row = sum([zr_r[i] for i in range(1, nz)], zr_r[0]) + own_normed_grad
    grad_initial = layer_norm_back(grad_normed_row, gain_row, hat_local, inverse_local)
    grad_align = (grad_middle + grad_initial).astype(BF16)
    galign_ref[0] = grad_align[:, :C]
    galign_ref[1] = grad_align[:, C:]
    stores[0].start()
    for p in range(PAIRS):
        bias_done(p)
    stores[1].start()
    gather_finish()
    gain_columns = [
        jnp.sum(identity * gains[i : i + 1], axis=1, keepdims=True) for i in range(2)
    ]

    def gain_gradient(part, weights):
        column_sum = jnp.sum(part * weights, axis=1, keepdims=True)
        return jnp.sum(identity * column_sum, axis=0, keepdims=True)

    wait_all(oc_r, 10, ns)
    final = oc_r[...].reshape(C, 2 * W)
    part = final[:, 0 : 2 * C + 2 * DH]
    gcolp_ref[...] = part * gain_columns[1]
    gcolo_ref[...] = final[:, 2 * C + 2 * DH : 3 * C + 2 * DH]
    ggains_ref[1:2, :] = gain_gradient(part, colp)
    stores[5].start()
    stores[6].start()

    wait_all(o_r, 8, ns)
    final = o_r[...].reshape(C, 3 * W)
    part = final[:, 0 : 4 * C]
    growp_ref[...] = part * gain_columns[0]
    growo_ref[...] = final[:, 4 * C : 5 * C]
    stores[3].start()
    stores[4].start()
    ggains_ref[0:1, :] = gain_gradient(part, rowp)
    stores[2].start()
    for store in stores:
        store.wait()


def store_all(*refs):
    count = (len(refs) - 1) // 2
    semaphores = refs[-1]
    copies = [
        pltpu.make_async_copy(refs[i], refs[count + i], semaphores.at[i]) for i in range(count)
    ]
    for copy in copies:
        copy.start()
    for copy in copies:
        copy.wait()


def finish(arrays):
    arrays = pl.pallas_call(
        store_all,
        out_shape=tuple(jax.ShapeDtypeStruct(a.shape, a.dtype) for a in arrays),
        in_specs=[pl.BlockSpec(memory_space=pltpu.VMEM)] * len(arrays),
        out_specs=(pl.BlockSpec(memory_space=pltpu.HBM),) * len(arrays),
        scratch_shapes=[pltpu.SemaphoreType.DMA((len(arrays),))],
    )(*arrays)
    return (arrays[0], jnp.swapaxes(arrays[1], 1, 2)) + tuple(arrays[2:])


def solution(mesh):
    seq_devices = mesh.shape["seq"]
    res_devices = mesh.shape["res"]
    nx = 4 if seq_devices == 64 else 2
    ny = seq_devices // (2 * nx)
    nz = res_devices
    res = seq_devices
    keys = nz * res
    block = keys // seq_devices
    half = 2 * res

    def local(
        alignment,
        cotangent,
        pair_bias,
        norm_gains,
        row_project,
        row_output,
        column_project,
        column_output,
        residue_mask,
        sequence_mask,
    ):
        ns = seq_devices
        chunk = C // ns
        outs = pl.pallas_call(
            functools.partial(kernel, (ny, nx, nz)),
            out_shape=(
                jax.ShapeDtypeStruct((L, res, C), BF16),
                jax.ShapeDtypeStruct((H, block, res), F32),
                jax.ShapeDtypeStruct((2, C), F32),
                jax.ShapeDtypeStruct((C, 4 * C), F32),
                jax.ShapeDtypeStruct((C, C), F32),
                jax.ShapeDtypeStruct((C, 2 * C + 2 * DH), F32),
                jax.ShapeDtypeStruct((C, C), F32),
            ),
            in_specs=[pl.BlockSpec(memory_space=pltpu.HBM)] * 10,
            out_specs=(pl.BlockSpec(memory_space=pltpu.HBM),) * 7,
            scratch_shapes=[
                pltpu.VMEM((nz, res + 8, W), F32),
                pltpu.VMEM((ns, 1, 2 * W), F32),
                pltpu.VMEM((ns, 1, 2 * W), F32),
                pltpu.VMEM((ns, 1, W), F32),
                pltpu.VMEM((ns, 1, W), F32),
                pltpu.VMEM((ns, 1, W), F32),
                pltpu.VMEM((ns, 1, W), F32),
                pltpu.VMEM((PAIRS, keys, half), F32),
                pltpu.VMEM((PAIRS, keys, 2 * half), F32),
                pltpu.VMEM((PAIRS, keys, 2 * half), BF16),
                pltpu.VMEM((PAIRS, keys, 2 * half), BF16),
                pltpu.VMEM((PAIRS, ny, nx, 2, block, half), F32),
                pltpu.VMEM((PAIRS, ny, nx, block, half), F32),
                pltpu.VMEM((PAIRS, nx, ny, block, half), F32),
                pltpu.VMEM((PAIRS, nx, ny, block, half), F32),
                pltpu.VMEM((PAIRS, ny, block, half), F32),
                pltpu.VMEM((PAIRS, ny, block, half), F32),
                pltpu.VMEM((nz, res, W), F32),
                pltpu.VMEM((nz, res, W), F32),
                pltpu.VMEM((ns, chunk, 2 * W), F32),
                pltpu.VMEM((ns, chunk, 2 * W), F32),
                pltpu.VMEM((ns, chunk, 3 * W), F32),
                pltpu.VMEM((ns, chunk, 3 * W), F32),
                pltpu.VMEM((chunk, 3 * W), F32),
                pltpu.VMEM((nz, chunk, 3 * W), F32),
                pltpu.VMEM((ns, chunk, 3 * W), F32),
                pltpu.VMEM((chunk, 2 * W), F32),
                pltpu.VMEM((nz, chunk, 2 * W), F32),
                pltpu.VMEM((ns, chunk, 2 * W), F32),
                pltpu.VMEM((L, res, C), BF16),
                pltpu.VMEM((L, res, C), BF16),
                pltpu.VMEM((H, res, keys), BF16),
                pltpu.VMEM((2, C), F32),
                pltpu.VMEM((C, 4 * C), F32),
                pltpu.VMEM((C, C), F32),
                pltpu.VMEM((C, 2 * C + 2 * DH), F32),
                pltpu.VMEM((C, C), F32),
                pltpu.VMEM((1, res), jnp.int32),
                pltpu.VMEM((1, L), jnp.int32),
                pltpu.SemaphoreType.DMA((11,)),
                pltpu.SemaphoreType.DMA((11,)),
                pltpu.SemaphoreType.DMA((3, PAIRS)),
                pltpu.SemaphoreType.DMA((3, PAIRS)),
                pltpu.SemaphoreType.DMA((10,)),
                pltpu.SemaphoreType.DMA((8,)),
                pltpu.SemaphoreType.DMA((8,)),
                pltpu.VMEM((L, res, C), BF16),
                pltpu.VMEM((H, block, res), F32),
                pltpu.VMEM((2, C), F32),
                pltpu.VMEM((C, 4 * C), F32),
                pltpu.VMEM((C, C), F32),
                pltpu.VMEM((C, 2 * C + 2 * DH), F32),
                pltpu.VMEM((C, C), F32),
                pltpu.SemaphoreType.DMA((7,)),
            ],
            compiler_params=pltpu.CompilerParams(
                collective_id=0, has_side_effects=True, vmem_limit_bytes=64 * 1024 * 1024
            ),
        )(
            alignment,
            cotangent,
            pair_bias,
            norm_gains,
            row_project,
            row_output,
            column_project,
            column_output,
            residue_mask[None],
            sequence_mask[None],
        )
        return finish(outs)

    placed = (
        P("seq", "res", None),
        P("seq", "res", None),
        P(None, "res", None),
        P(),
        P(),
        P(),
        P(),
        P(),
        P("res"),
        P("seq"),
    )
    return jax.shard_map(
        local,
        mesh=mesh,
        in_specs=placed,
        out_specs=(P("seq", "res", None), P(None, "res", "seq"), P(), P(), P(), P(), P()),
        check_vma=False,
    )
```

```python
import functools
import jax
import jax.numpy as jnp
from jax import lax
from jax.experimental import pallas as pl
from jax.experimental.pallas import tpu as pltpu
from jax.sharding import PartitionSpec as P

C = 64
H = 8
DH = 8
L = 2
PAIRS = 4
W = 128
EPSILON = 1e-05
MASKED = 1000000000.0
F32 = jnp.float32
BF16 = jnp.bfloat16
MESH = pl.DeviceIdType.MESH
NN = (((1,), (0,)), ((), ()))
NT = (((1,), (1,)), ((), ()))
TN = (((0,), (0,)), ((), ()))


def dot(a, b, dims=NN):
    return lax.dot_general(
        a, b, dims, precision=lax.Precision.HIGHEST, preferred_element_type=F32
    )


def dot1(a, b, dims=NN):
    return lax.dot_general(a, b, dims, preferred_element_type=F32)


def split2(a):
    high = a.astype(BF16)
    return high, (a - high.astype(F32)).astype(BF16)


def split3(a):
    high = a.astype(BF16)
    rest = a - high.astype(F32)
    middle = rest.astype(BF16)
    return high, middle, (rest - middle.astype(F32)).astype(BF16)


def dot3(a, b, dims=NN):
    ah, al = split2(a)
    bh, bl = split2(b)
    return dot1(ah, bh, dims) + (dot1(ah, bl, dims) + dot1(al, bh, dims))


def products(first, second):
    a1, a2, a3 = first
    b1, b2, b3 = second
    a12 = jnp.concatenate([a1, a2], axis=1)
    a13 = jnp.concatenate([a1, a3], axis=1)
    return dot1(a12, jnp.concatenate([b1, b1], axis=0)) + (
        dot1(a12, jnp.concatenate([b2, b2], axis=0)) + dot1(a13, jnp.concatenate([b3, b1], axis=0))
    )


def pick(values, ones, dims=NN):
    ones = ones.astype(BF16)
    axis = dims[0][1][0]
    return dot1(
        jnp.concatenate(split2(values), axis=1), jnp.concatenate([ones, ones], axis=axis), dims
    )


def exact(values, fixed):
    fixed = fixed.astype(BF16)
    return dot1(
        jnp.concatenate(split3(values), axis=1), jnp.concatenate([fixed, fixed, fixed], axis=0)
    )


def outer3(left, right):
    lh, ll = left
    rh, rl = right
    both = dot1(lh, jnp.concatenate([rh, rl], axis=0), NT)
    count = rh.shape[0]
    return both[:, :count] + (both[:, count:] + dot1(ll, rh, NT))


def iota(shape, axis):
    return lax.broadcasted_iota(jnp.int32, shape, axis)


def ones_where(condition):
    return jnp.where(condition, 1.0, 0.0).astype(F32)


def twice(row):
    return jnp.concatenate([row, row], axis=1)


def fold(row):
    return row + jnp.concatenate([row[:, C:], row[:, :C]], axis=1)


def block_diagonal(weights):
    zero = jnp.zeros_like(weights)
    return jnp.concatenate(
        [jnp.concatenate([weights, zero], axis=1), jnp.concatenate([zero, weights], axis=1)], axis=0
    )


def diagonal_sum(full):
    return full[:C, :C] + full[C:, C:]


def kernel(
    sizes,
    align_hbm,
    cot_hbm,
    bias_hbm,
    gains_hbm,
    rowp_hbm,
    rowo_hbm,
    colp_hbm,
    colo_hbm,
    rmask_hbm,
    smask_hbm,
    galign_hbm,
    gbias_hbm,
    ggains_hbm,
    growp_hbm,
    growo_hbm,
    gcolp_hbm,
    gcolo_hbm,
    xall,
    gsend,
    grecv,
    msend,
    mrecv,
    bsend,
    brecv,
    bias_t,
    exps,
    exps_high,
    exps_low,
    bias_s,
    core_r,
    x_s,
    x_r,
    y_s,
    y_r,
    zr_s,
    zr_r,
    pc_s,
    pc_r,
    pr_s,
    pr_r,
    t_s,
    t_r,
    o_r,
    tc_s,
    tc_r,
    oc_r,
    align_ref,
    cot_ref,
    bias_ref,
    gains_ref,
    rowp_ref,
    rowo_ref,
    colp_ref,
    colo_ref,
    rmask_ref,
    smask_ref,
    send_sem,
    recv_sem,
    bias_send,
    bias_recv,
    load_sem,
    gather_send,
    gather_recv,
    galign_ref,
    gbias_ref,
    ggains_ref,
    growp_ref,
    growo_ref,
    gcolp_ref,
    gcolo_ref,
    store_sem,
):
    ny, nx, nz = sizes
    ns = ny * nx * 2
    res = ns
    keys = nz * res
    wide = 4 * res
    half = 2 * res
    block = keys // ns
    me = lax.axis_index("seq")
    mz = lax.axis_index("res")
    core = lax.rem(me, 2)
    mx = lax.rem(me // 2, nx)
    my = me // (2 * nx)
    scaling = DH ** (-0.5)

    sources = (
        align_hbm,
        rmask_hbm,
        smask_hbm,
        cot_hbm,
        gains_hbm,
        rowp_hbm,
        rowo_hbm,
        bias_hbm,
        colp_hbm,
        colo_hbm,
    )
    targets = (
        align_ref,
        rmask_ref,
        smask_ref,
        cot_ref,
        gains_ref,
        rowp_ref,
        rowo_ref,
        bias_ref,
        colp_ref,
        colo_ref,
    )
    loads = [
        pltpu.make_async_copy(source, target, load_sem.at[i])
        for i, (source, target) in enumerate(zip(sources, targets))
    ]
    for load in loads:
        load.start()

    barrier = pltpu.get_barrier_semaphore()

    def greet_seq(i, carry):
        pl.semaphore_signal(
            barrier, inc=1, device_id=(lax.rem(me + i, ns), mz), device_id_type=MESH
        )
        return carry

    def greet_res(i, carry):
        pl.semaphore_signal(
            barrier, inc=1, device_id=(me, lax.rem(mz + i, nz)), device_id_type=MESH
        )
        return carry

    lax.fori_loop(1, nz, greet_res, 0)
    lax.fori_loop(ns // 4, ns, greet_seq, 0)
    lax.fori_loop(1, ns // 4, greet_seq, 0)

    stores = [
        pltpu.make_async_copy(source, target, store_sem.at[i])
        for i, (source, target) in enumerate(
            (
                (galign_ref, galign_hbm),
                (gbias_ref, gbias_hbm),
                (ggains_ref, ggains_hbm),
                (growp_ref, growp_hbm),
                (growo_ref, growo_hbm),
                (gcolp_ref, gcolp_hbm),
                (gcolo_ref, gcolo_hbm),
            )
        )
    ]

    def to_seq(source, target, which):
        def one(i, carry):
            j = lax.rem(me + i, ns)
            pltpu.make_async_remote_copy(
                src_ref=source(j),
                dst_ref=target.at[me],
                send_sem=send_sem.at[which],
                recv_sem=recv_sem.at[which],
                device_id=(j, mz),
                device_id_type=MESH,
            ).start()
            return carry

        lax.fori_loop(ns // 4, ns, one, 0)
        lax.fori_loop(1, ns // 4, one, 0)

    def to_res(source, target, which):
        def one(i, carry):
            j = lax.rem(mz + i, nz)
            pltpu.make_async_remote_copy(
                src_ref=source(j),
                dst_ref=target.at[mz],
                send_sem=send_sem.at[which],
                recv_sem=recv_sem.at[which],
                device_id=(me, j),
                device_id_type=MESH,
            ).start()
            return carry

        lax.fori_loop(1, nz, one, 0)

    def wait(ref, semaphore):
        pltpu.make_async_copy(ref, ref, semaphore).wait()

    def wait_all(buffer, which, count):
        part = buffer.at[pl.ds(0, count - 1)]
        wait(part, recv_sem.at[which])
        wait(part, send_sem.at[which])

    def keep(source, target, at):
        target[pl.ds(at, 1)] = source[pl.ds(at, 1)]

    ring = (3, nz - 3, 2, nz - 2, 1, nz - 1)
    cut = (res + 8) // 16 * 8

    def gather_copy(step):
        return pltpu.make_async_remote_copy(
            src_ref=xall.at[mz],
            dst_ref=xall.at[mz],
            send_sem=gather_send.at[step],
            recv_sem=gather_recv.at[step],
            device_id=(me, lax.rem(mz + step, nz)),
            device_id_type=MESH,
        )

    def gather_relay(step, rows, semaphore):
        part = xall.at[lax.rem(mz + nz - step, nz), rows]
        return pltpu.make_async_remote_copy(
            src_ref=part,
            dst_ref=part,
            send_sem=gather_send.at[semaphore],
            recv_sem=gather_recv.at[semaphore],
            device_id=(me, lax.rem(mz + (nz // 2 - step) + nz, nz)),
            device_id_type=MESH,
        )

    relays = ((3, pl.ds(0, cut), 0), (nz - 3, pl.ds(cut, res + 8 - cut), 4))

    def gather_start():
        if nz != 8:
            to_res(lambda j: xall.at[mz], xall, 0)
            return
        for step in ring:
            gather_copy(step).start()

    def gather_pass_on():
        if nz != 8:
            return
        for step, rows, semaphore in relays:
            gather_copy(step).wait_recv()
            gather_relay(step, rows, semaphore).start()

    def gather_wait():
        if nz != 8:
            wait_all(xall, 0, nz)
            return
        for step in ring[2:]:
            gather_copy(step).wait_recv()
        for relay in relays:
            gather_relay(*relay).wait_recv()

    def gather_finish():
        if nz != 8:
            return
        for step in ring:
            gather_copy(step).wait_send()
        for relay in relays:
            gather_relay(*relay).wait_send()

    for load in loads[:4]:
        load.wait()
    align = align_ref[...].astype(F32)
    initial = jnp.concatenate([align[0], align[1]], axis=1)
    cot = cot_ref[...].astype(F32)
    top_local = jnp.concatenate([cot[0], cot[1]], axis=1)
    averaging = ones_where(iota((W, W), 0) // C == iota((W, W), 1) // C) * (1.0 / C)

    def layer_norm(values):
        centred = values - exact(values, averaging)
        spread = exact(centred * centred, averaging)
        inverse = lax.rsqrt(spread + EPSILON)
        return centred * inverse, inverse

    def layer_norm_back(grad_normed, gain, hat, inverse):
        scaled = grad_normed * gain
        rows = scaled.shape[0]
        means = exact(jnp.concatenate([scaled, scaled * hat], axis=0), averaging)
        return inverse * (scaled - means[:rows] - hat * means[rows:])

    hat_local, inverse_local = layer_norm(initial)
    xall[mz, 0:res, :] = hat_local
    xall[mz, res : res + 8, :] = jnp.broadcast_to(
        jnp.concatenate([rmask_ref[...].astype(F32), jnp.zeros((1, W - res), F32)], axis=1), (8, W)
    )
    present_pair = smask_ref[...].astype(F32)
    present_row = jnp.concatenate(
        [jnp.broadcast_to(present_pair[:, i : i + 1], (1, C)) for i in range(L)], axis=1
    )
    gsend[:, 0, 0:W] = top_local
    gsend[:, 0, W : 2 * W] = jnp.broadcast_to(present_row, (res, W))

    pl.semaphore_wait(barrier, ns + nz - 2)
    gather_start()
    to_seq(lambda j: gsend.at[j], grecv, 1)
    keep(gsend, grecv, me)

    for load in loads[4:]:
        load.wait()
    gains = gains_ref[...]
    gain_row = twice(gains[0:1])
    gain_col = twice(gains[1:2])

    lane = iota((C, W), 1)
    column = (lane // 32) * 16 + lane % 16
    chosen = [
        ones_where((iota((C, W), 0) == column) & ((lane // 16) % 2 == s)) for s in range(L)
    ]

    def spread_columns(weights):
        return jnp.concatenate([dot(weights, chosen[0]), dot(weights, chosen[1])], axis=0)

    rowp = rowp_ref[...]
    query_w = spread_columns(rowp[:, 0:C])
    key_w = spread_columns(rowp[:, C : 2 * C])
    value_w = spread_columns(rowp[:, 2 * C : 3 * C])
    gate_w = spread_columns(rowp[:, 3 * C :])
    rowo = rowo_ref[...]
    out_w = jnp.concatenate([dot(chosen[0], rowo, TN), dot(chosen[1], rowo, TN)], axis=1)
    memory_w = jnp.concatenate([key_w, value_w], axis=1)

    normed_local = hat_local * gain_row
    queries = dot(normed_local, query_w) * scaling
    gate_row = jax.nn.sigmoid(dot(normed_local, gate_w))

    gather_pass_on()
    for p in range(PAIRS):
        pair = bias_ref[2 * p : 2 * p + 2].astype(F32).reshape(half, keys)
        bias_t[p] = pair.T

    mine = ones_where(iota((32, wide), 0) // DH == iota((32, wide), 1) // res)
    nothing = jnp.zeros((32, wide), BF16)
    group = iota((keys, W), 1) // 32

    def heads_apart(rows):
        flat = rows.T
        flat = jnp.concatenate([flat, flat, flat, flat], axis=1)
        return [flat[32 * p : 32 * p + 32] * mine for p in range(PAIRS)]

    def placed(part, p):
        return jnp.concatenate([part if i == p else nothing for i in range(PAIRS)], axis=0)

    def turns(part):
        part = part.astype(F32)
        return [part] + [pltpu.roll(part, 32 * i, 1) for i in range(1, PAIRS)]

    def lanes_of(p, *parts):
        found = parts[-1][(len(parts) - 1 - p) % PAIRS]
        for i in reversed(range(len(parts) - 1)):
            found = jnp.where(group == i, parts[i][(i - p) % PAIRS], found)
        return found.astype(BF16)

    query_parts = [split3(apart) for apart in heads_apart(queries)]
    query_stacks = [
        jnp.concatenate([q1, q2, q1, q2, q3, q1, nothing, nothing], axis=0)
        for q1, q2, q3 in query_parts
    ]

    def heads_together(apart):
        kept = apart * mine
        both = kept[:, :half] + kept[:, half:]
        return both[:, :res] + both[:, res:]

    identity = ones_where(iota((C, C), 0) == iota((C, C), 1))
    colp = colp_ref[...]
    colo = colo_ref[...]
    entry = iota((C + 2 * DH + C, C), 0)
    entry_lane = iota((C + 2 * DH + C, C), 1)
    key_col_w = block_diagonal(dot(colp, ones_where(entry == C + entry_lane % DH)))
    value_col_w = block_diagonal(dot(colp, ones_where(entry == C + DH + entry_lane % DH)))
    gate_col_w = block_diagonal(dot(colp, ones_where(entry == C + 2 * DH + entry_lane)))
    query_col_w = block_diagonal(colp[:, 0:C])
    out_col_w = block_diagonal(colo)
    column_w = jnp.concatenate([key_col_w, value_col_w, gate_col_w], axis=1)
    head_sum = ones_where(iota((W, W), 0) // DH == iota((W, W), 1) // DH)

    gather_wait()
    hat_all = xall[:, 0:res, :].reshape(keys, W)
    normed_all = hat_all * gain_row
    memory = products(split3(normed_all), split3(memory_w))
    key_rows = memory[:, :W]
    value_rows = memory[:, W:]
    value_flat = value_rows.T
    mask_flat = jnp.concatenate([xall[z, res : res + 8, :] for z in range(nz)], axis=0).T
    key_bias = jnp.concatenate(
        [MASKED * (mask_flat[:res, 8 * z : 8 * z + 1] - 1.0) for z in range(nz)], axis=0
    )
    t1, t2, t3 = [turns(part) for part in split3(key_rows)]
    value_high, value_low = split2(value_flat)

    totals = []
    mixed = []
    for p in range(PAIRS):
        key_stack = jnp.concatenate([lanes_of(p, t1, t1, t2, t2), lanes_of(p, t1, t3)], axis=1)
        scores = dot1(key_stack, query_stacks[p])
        scores = scores + twice(bias_t[p]) + key_bias
        peak = jnp.max(scores, axis=0, keepdims=True)
        exponent = jnp.exp(scores - peak)
        exps[p] = exponent
        inverse_total = 1.0 / jnp.sum(exponent, axis=0, keepdims=True)
        totals.append(inverse_total)
        eh, el = split2(exponent)
        exps_high[p] = eh
        exps_low[p] = el
        vh = value_high[32 * p : 32 * p + 32]
        vl = value_low[32 * p : 32 * p + 32]
        apart = dot1(vh, eh) + (dot1(vl, eh) + dot1(vh, el))
        mixed.append(heads_together(apart * inverse_total))
    mixture = jnp.concatenate(mixed, axis=0).T
    gated = gate_row * mixture
    middle = initial + dot(gated, out_w)
    msend[:, 0, :] = middle
    to_seq(lambda j: msend.at[j], mrecv, 2)
    keep(msend, mrecv, me)

    key_flat = key_rows.T
    key_high, key_low = split2(key_flat)

    wait_all(grecv, 1, ns)
    top = grecv[:, 0, 0:W]
    present = grecv[:, 0, W : 2 * W]
    counted = jnp.sum(fold(jnp.sum(present, axis=0, keepdims=True)), axis=1, keepdims=True) * (
        1.0 / W
    )
    inverse_count = 1.0 / counted
    grad_gated_col = dot(top, out_col_w, NT)

    wait_all(mrecv, 2, ns)
    hat_col, inverse_col = layer_norm(mrecv[:, 0, :])
    normed_col = hat_col * gain_col
    mean_normed = fold(jnp.sum(present * normed_col, axis=0, keepdims=True)) * inverse_count
    queries_col = dot(mean_normed, query_col_w) * scaling
    projected = dot(normed_col, column_w)
    key_col = projected[:, 0:W]
    value_col = projected[:, W : 2 * W]
    gate_col = jax.nn.sigmoid(projected[:, 2 * W :])
    scores_col = exact(key_col * queries_col, head_sum) + MASKED * (present - 1.0)
    peak_row = jnp.max(scores_col, axis=0, keepdims=True)
    peak_row = jnp.maximum(peak_row, jnp.concatenate([peak_row[:, C:], peak_row[:, :C]], axis=1))
    exp_col = jnp.exp(scores_col - peak_row)
    weights_col = exp_col * (1.0 / fold(jnp.sum(exp_col, axis=0, keepdims=True)))
    mixture_col = fold(jnp.sum(weights_col * value_col, axis=0, keepdims=True))
    grad_mixture_col = fold(jnp.sum(gate_col * grad_gated_col, axis=0, keepdims=True))
    grad_gate_col = grad_gated_col * mixture_col * gate_col * (1.0 - gate_col)
    grad_weights_col = exact(value_col * grad_mixture_col, head_sum)
    inner_col = fold(jnp.sum(weights_col * grad_weights_col, axis=0, keepdims=True))
    grad_scores_col = weights_col * (grad_weights_col - inner_col)
    grad_query_col = fold(jnp.sum(grad_scores_col * key_col, axis=0, keepdims=True)) * scaling
    grad_key_col = grad_scores_col * queries_col
    grad_value_col = weights_col * grad_mixture_col
    grad_mean = dot(grad_query_col, query_col_w, NT)
    grad_projected = jnp.concatenate([grad_key_col, grad_value_col, grad_gate_col], axis=1)
    grad_normed_col = present * inverse_count * grad_mean + dot(grad_projected, column_w, NT)
    grad_middle_col = top + layer_norm_back(grad_normed_col, gain_col, hat_col, inverse_col)
    bsend[:, 0, :] = grad_middle_col
    to_seq(lambda j: bsend.at[j], brecv, 3)
    keep(bsend, brecv, me)

    pack_lane = iota((C, 2 * W), 1)
    pack_row = iota((C, 2 * W), 0)
    grad_full = dot(hat_col, grad_projected, TN)
    mean_hat = fold(jnp.sum(present * hat_col, axis=0, keepdims=True)) * inverse_count
    mean_column = jnp.sum(identity * mean_hat[:, :C], axis=1, keepdims=True)
    grad_col_parts = jnp.concatenate(
        [
            mean_column * grad_query_col[:, :C],
            diagonal_sum(grad_full[:, 0:W]),
            diagonal_sum(grad_full[:, W : 2 * W]),
            diagonal_sum(grad_full[:, 2 * W :]),
            diagonal_sum(dot(gate_col * mixture_col, top, TN)),
        ],
        axis=1,
    )
    placing = jnp.concatenate(
        [
            ones_where(pack_lane == pack_row),
            ones_where(pack_lane == C + pack_row % DH),
            ones_where(pack_lane == C + DH + pack_row % DH),
            ones_where(pack_lane == C + 2 * DH + pack_row),
            ones_where(pack_lane == 2 * C + 2 * DH + pack_row),
        ],
        axis=0,
    )
    pack = pick(grad_col_parts, placing)
    pc_s[...] = pack.reshape(ns, C // ns, 2 * W)
    to_seq(lambda j: pc_s.at[j], pc_r, 4)
    keep(pc_s, pc_r, me)

    v1, v2 = [turns(part) for part in split2(value_rows)]
    hat_high, hat_low = split2(hat_all.T)
    value_stacks = [lanes_of(p, v1, v2, v1) for p in range(PAIRS)]

    wait_all(brecv, 3, ns)
    grad_middle = brecv[:, 0, :]
    grad_gated = dot(grad_middle, out_w, NT)
    grad_gate = grad_gated * mixture * gate_row * (1.0 - gate_row)
    grads_apart = heads_apart(grad_gated * gate_row)
    grad_out_w = dot3(gated, grad_middle, TN)
    grad_rowo = dot(chosen[0], grad_out_w[:, :C]) + dot(chosen[1], grad_out_w[:, C:])

    def bias_core(p):
        return pltpu.make_async_remote_copy(
            src_ref=bias_s.at[p, :, :, 1 - core],
            dst_ref=core_r.at[p],
            send_sem=bias_send.at[0, p],
            recv_sem=bias_recv.at[0, p],
            device_id=(me + 1 - 2 * core, mz),
            device_id_type=MESH,
        )

    def bias_to_x(p):
        bias_core(p).wait()
        x_s[p] = jnp.swapaxes(bias_s[p, :, :, core] + core_r[p], 0, 1)

        def one(i, carry):
            j = lax.rem(mx + i, nx)
            pltpu.make_async_remote_copy(
                src_ref=x_s.at[p, j],
                dst_ref=x_r.at[p, mx],
                send_sem=bias_send.at[1, p],
                recv_sem=bias_recv.at[1, p],
                device_id=((my * nx + j) * 2 + core, mz),
                device_id_type=MESH,
            ).start()
            return carry

        lax.fori_loop(1, nx, one, 0)
        x_r[p, pl.ds(mx, 1)] = x_s[p, pl.ds(mx, 1)]

    def bias_to_y(p):
        part = x_r.at[p, pl.ds(0, nx - 1)]
        wait(part, bias_recv.at[1, p])
        wait(part, bias_send.at[1, p])
        y_s[p] = sum([x_r[p, i] for i in range(1, nx)], x_r[p, 0])

        def one(i, carry):
            j = lax.rem(my + i, ny)
            pltpu.make_async_remote_copy(
                src_ref=y_s.at[p, j],
                dst_ref=y_r.at[p, my],
                send_sem=bias_send.at[2, p],
                recv_sem=bias_recv.at[2, p],
                device_id=((j * nx + mx) * 2 + core, mz),
                device_id_type=MESH,
            ).start()
            return carry

        lax.fori_loop(1, ny, one, 0)
        y_r[p, pl.ds(my, 1)] = y_s[p, pl.ds(my, 1)]

    def bias_done(p):
        part = y_r.at[p, pl.ds(0, ny - 1)]
        wait(part, bias_recv.at[2, p])
        wait(part, bias_send.at[2, p])
        total = sum([y_r[p, i] for i in range(1, ny)], y_r[p, 0])
        gbias_ref[2 * p] = total[:, :res]
        gbias_ref[2 * p + 1] = total[:, res:]

    score_parts = []
    value_parts = []
    grad_queries = []
    for p in range(PAIRS):
        gh, gl = split2(grads_apart[p] * totals[p])
        grad_weights = dot1(value_stacks[p], jnp.concatenate([gh, gh, gl, nothing], axis=0))
        exponent = exps[p]
        inner = jnp.sum(exponent * grad_weights, axis=0, keepdims=True) * totals[p]
        grad_scores = exponent * (grad_weights - inner)
        bias_s[p] = (grad_scores[:, :half] + grad_scores[:, half:]).reshape(
            ny, nx, 2, block, half
        )
        bias_core(p).start()
        sh, sl = split2(grad_scores)
        score_parts.append((sh, sl))
        value_parts.append((gh, gl))
        kh = key_high[32 * p : 32 * p + 32]
        kl = key_low[32 * p : 32 * p + 32]
        grad_queries.append(
            heads_together(dot1(kh, sh) + (dot1(kl, sh) + dot1(kh, sl)))
        )

    empty = jnp.zeros((W, wide), BF16)

    def outer_all(lefts, rights):
        left = jnp.concatenate([part for pair in lefts for part in pair], axis=1)
        highs = [placed(rh, p) for p, (rh, _) in enumerate(rights)]
        lows = [placed(rl, p) for p, (_, rl) in enumerate(rights)]
        right = jnp.concatenate(
            [
                jnp.concatenate([part for high in highs for part in (high, high)], axis=1),
                jnp.concatenate([part for low in lows for part in (low, empty)], axis=1),
            ],
            axis=0,
        )
        both = dot1(left, right, NT)
        return both[:, :W] + both[:, W:]

    grad_keys = outer_all(score_parts, [parts[:2] for parts in query_parts])
    grad_values = outer_all([(exps_high[p], exps_low[p]) for p in range(PAIRS)], value_parts)

    grad_memory = jnp.concatenate([grad_keys, grad_values], axis=1)
    grad_query = jnp.concatenate(grad_queries, axis=0).T * scaling
    own_grads = jnp.concatenate([grad_query, grad_gate], axis=1)
    gh, gl = split2(grad_memory)
    grad_memory_w = dot1(hat_high, gh) + (dot1(hat_high, gl) + dot1(hat_low, gh))
    grad_own_w = dot3(hat_local, own_grads, TN)
    grad_parts = (
        grad_own_w[:, :W],
        grad_memory_w[:, :W],
        grad_memory_w[:, W:],
        grad_own_w[:, W:],
    )
    gathered = pick(
        jnp.concatenate([part[:C] for part in grad_parts], axis=0), chosen[0], NT
    ) + pick(jnp.concatenate([part[C:] for part in grad_parts], axis=0), chosen[1], NT)
    pack_row_part = jnp.concatenate(
        [gathered[i * C : (i + 1) * C] for i in range(4)] + [grad_rowo, jnp.zeros((C, C), F32)],
        axis=1,
    )
    pr_s[...] = pack_row_part.reshape(ns, C // ns, 3 * W)
    to_seq(lambda j: pr_s.at[j], pr_r, 6)
    keep(pr_s, pr_r, me)

    for p in range(PAIRS):
        bias_to_x(p)
    wait_all(pc_r, 4, ns)
    tc_s[...] = jnp.sum(pc_r[...], axis=0)
    to_res(lambda j: tc_s, tc_r, 9)
    tc_r[pl.ds(mz, 1)] = tc_s[...][None]
    own_normed_grad = dot(own_grads, jnp.concatenate([query_w, gate_w], axis=1), NT)
    zr_s[...] = dot3(grad_memory, memory_w, NT).reshape(nz, res, W)
    keep(zr_s, zr_r, mz)
    wait_all(tc_r, 9, nz)
    oc_r[me] = sum([tc_r[i] for i in range(1, nz)], tc_r[0])
    to_seq(lambda j: oc_r.at[me], oc_r, 10)

    wait_all(pr_r, 6, ns)
    t_s[...] = jnp.sum(pr_r[...], axis=0)
    to_res(lambda j: t_s, t_r, 7)
    t_r[pl.ds(mz, 1)] = t_s[...][None]
    to_res(lambda j: zr_s.at[j], zr_r, 5)
    for p in range(PAIRS):
        bias_to_y(p)

    wait_all(t_r, 7, nz)
    o_r[me] = sum([t_r[i] for i in range(1, nz)], t_r[0])
    to_seq(lambda j: o_r.at[me], o_r, 8)

    wait_all(zr_r, 5, nz)
    grad_normed_row = sum([zr_r[i] for i in range(1, nz)], zr_r[0]) + own_normed_grad
    grad_initial = layer_norm_back(grad_normed_row, gain_row, hat_local, inverse_local)
    grad_align = (grad_middle + grad_initial).astype(BF16)
    galign_ref[0] = grad_align[:, :C]
    galign_ref[1] = grad_align[:, C:]
    stores[0].start()
    for p in range(PAIRS):
        bias_done(p)
    stores[1].start()
    gather_finish()
    gain_columns = [
        jnp.sum(identity * gains[i : i + 1], axis=1, keepdims=True) for i in range(2)
    ]

    def gain_gradient(part, weights):
        column_sum = jnp.sum(part * weights, axis=1, keepdims=True)
        return jnp.sum(identity * column_sum, axis=0, keepdims=True)

    wait_all(oc_r, 10, ns)
    final = oc_r[...].reshape(C, 2 * W)
    part = final[:, 0 : 2 * C + 2 * DH]
    gcolp_ref[...] = part * gain_columns[1]
    gcolo_ref[...] = final[:, 2 * C + 2 * DH : 3 * C + 2 * DH]
    ggains_ref[1:2, :] = gain_gradient(part, colp)
    stores[5].start()
    stores[6].start()

    wait_all(o_r, 8, ns)
    final = o_r[...].reshape(C, 3 * W)
    part = final[:, 0 : 4 * C]
    growp_ref[...] = part * gain_columns[0]
    growo_ref[...] = final[:, 4 * C : 5 * C]
    stores[3].start()
    stores[4].start()
    ggains_ref[0:1, :] = gain_gradient(part, rowp)
    stores[2].start()
    for store in stores:
        store.wait()


def store_all(*refs):
    count = (len(refs) - 1) // 2
    semaphores = refs[-1]
    copies = [
        pltpu.make_async_copy(refs[i], refs[count + i], semaphores.at[i]) for i in range(count)
    ]
    for copy in copies:
        copy.start()
    for copy in copies:
        copy.wait()


def finish(arrays):
    arrays = pl.pallas_call(
        store_all,
        out_shape=tuple(jax.ShapeDtypeStruct(a.shape, a.dtype) for a in arrays),
        in_specs=[pl.BlockSpec(memory_space=pltpu.VMEM)] * len(arrays),
        out_specs=(pl.BlockSpec(memory_space=pltpu.HBM),) * len(arrays),
        scratch_shapes=[pltpu.SemaphoreType.DMA((len(arrays),))],
    )(*arrays)
    return (arrays[0], jnp.swapaxes(arrays[1], 1, 2)) + tuple(arrays[2:])


def solution(mesh):
    seq_devices = mesh.shape["seq"]
    res_devices = mesh.shape["res"]
    nx = 4 if seq_devices == 64 else 2
    ny = seq_devices // (2 * nx)
    nz = res_devices
    res = seq_devices
    keys = nz * res
    block = keys // seq_devices
    half = 2 * res

    def local(
        alignment,
        cotangent,
        pair_bias,
        norm_gains,
        row_project,
        row_output,
        column_project,
        column_output,
        residue_mask,
        sequence_mask,
    ):
        ns = seq_devices
        chunk = C // ns
        outs = pl.pallas_call(
            functools.partial(kernel, (ny, nx, nz)),
            out_shape=(
                jax.ShapeDtypeStruct((L, res, C), BF16),
                jax.ShapeDtypeStruct((H, block, res), F32),
                jax.ShapeDtypeStruct((2, C), F32),
                jax.ShapeDtypeStruct((C, 4 * C), F32),
                jax.ShapeDtypeStruct((C, C), F32),
                jax.ShapeDtypeStruct((C, 2 * C + 2 * DH), F32),
                jax.ShapeDtypeStruct((C, C), F32),
            ),
            in_specs=[pl.BlockSpec(memory_space=pltpu.HBM)] * 10,
            out_specs=(pl.BlockSpec(memory_space=pltpu.HBM),) * 7,
            scratch_shapes=[
                pltpu.VMEM((nz, res + 8, W), F32),
                pltpu.VMEM((ns, 1, 2 * W), F32),
                pltpu.VMEM((ns, 1, 2 * W), F32),
                pltpu.VMEM((ns, 1, W), F32),
                pltpu.VMEM((ns, 1, W), F32),
                pltpu.VMEM((ns, 1, W), F32),
                pltpu.VMEM((ns, 1, W), F32),
                pltpu.VMEM((PAIRS, keys, half), F32),
                pltpu.VMEM((PAIRS, keys, 2 * half), F32),
                pltpu.VMEM((PAIRS, keys, 2 * half), BF16),
                pltpu.VMEM((PAIRS, keys, 2 * half), BF16),
                pltpu.VMEM((PAIRS, ny, nx, 2, block, half), F32),
                pltpu.VMEM((PAIRS, ny, nx, block, half), F32),
                pltpu.VMEM((PAIRS, nx, ny, block, half), F32),
                pltpu.VMEM((PAIRS, nx, ny, block, half), F32),
                pltpu.VMEM((PAIRS, ny, block, half), F32),
                pltpu.VMEM((PAIRS, ny, block, half), F32),
                pltpu.VMEM((nz, res, W), F32),
                pltpu.VMEM((nz, res, W), F32),
                pltpu.VMEM((ns, chunk, 2 * W), F32),
                pltpu.VMEM((ns, chunk, 2 * W), F32),
                pltpu.VMEM((ns, chunk, 3 * W), F32),
                pltpu.VMEM((ns, chunk, 3 * W), F32),
                pltpu.VMEM((chunk, 3 * W), F32),
                pltpu.VMEM((nz, chunk, 3 * W), F32),
                pltpu.VMEM((ns, chunk, 3 * W), F32),
                pltpu.VMEM((chunk, 2 * W), F32),
                pltpu.VMEM((nz, chunk, 2 * W), F32),
                pltpu.VMEM((ns, chunk, 2 * W), F32),
                pltpu.VMEM((L, res, C), BF16),
                pltpu.VMEM((L, res, C), BF16),
                pltpu.VMEM((H, res, keys), BF16),
                pltpu.VMEM((2, C), F32),
                pltpu.VMEM((C, 4 * C), F32),
                pltpu.VMEM((C, C), F32),
                pltpu.VMEM((C, 2 * C + 2 * DH), F32),
                pltpu.VMEM((C, C), F32),
                pltpu.VMEM((1, res), jnp.int32),
                pltpu.VMEM((1, L), jnp.int32),
                pltpu.SemaphoreType.DMA((11,)),
                pltpu.SemaphoreType.DMA((11,)),
                pltpu.SemaphoreType.DMA((3, PAIRS)),
                pltpu.SemaphoreType.DMA((3, PAIRS)),
                pltpu.SemaphoreType.DMA((10,)),
                pltpu.SemaphoreType.DMA((8,)),
                pltpu.SemaphoreType.DMA((8,)),
                pltpu.VMEM((L, res, C), BF16),
                pltpu.VMEM((H, block, res), F32),
                pltpu.VMEM((2, C), F32),
                pltpu.VMEM((C, 4 * C), F32),
                pltpu.VMEM((C, C), F32),
                pltpu.VMEM((C, 2 * C + 2 * DH), F32),
                pltpu.VMEM((C, C), F32),
                pltpu.SemaphoreType.DMA((7,)),
            ],
            compiler_params=pltpu.CompilerParams(
                collective_id=0, has_side_effects=True, vmem_limit_bytes=64 * 1024 * 1024
            ),
        )(
            alignment,
            cotangent,
            pair_bias,
            norm_gains,
            row_project,
            row_output,
            column_project,
            column_output,
            residue_mask[None],
            sequence_mask[None],
        )
        return finish(outs)

    placed = (
        P("seq", "res", None),
        P("seq", "res", None),
        P(None, "res", None),
        P(),
        P(),
        P(),
        P(),
        P(),
        P("res"),
        P("seq"),
    )
    return jax.shard_map(
        local,
        mesh=mesh,
        in_specs=placed,
        out_specs=(P("seq", "res", None), P(None, "res", "seq"), P(), P(), P(), P(), P()),
        check_vma=False,
    )
```
